32 devices in a mesh: fsdp: 8 (over y, x, core), rep: 4 (over z).
Axes of the slice: x: 2, y: 2, z: 4, core: 2. Of those that a mesh axis runs over, the one named last changes fastest.
Arguments:
- tokens: bfloat16 [12288, 1600], P(('fsdp', 'rep')), may hold values from -41 to 41
- norm_gain: float32 [1600], replicated, may hold values from 0.1 to 1.9
- up_weight: bfloat16 [6400, 1600], P('fsdp'), may hold values from -0.15625 to 0.15625
- up_bias: bfloat16 [6400], P('fsdp'), may hold values from -3 to 3
- keep_mask: int32 [128], P(('fsdp', 'rep')), may hold values 0 or 1
- cotangent: bfloat16 [12288, 6400], P(('fsdp', 'rep')), may hold values from -6 to 6
Outputs:
- hidden: bfloat16 [12288, 6400], P(('fsdp', 'rep'))
- grad_in: bfloat16 [12288, 1600], P(('fsdp', 'rep'))
- grad_weight: float32 [6400, 1600], P('fsdp')
- grad_bias: float32 [6400], P('fsdp')
- grad_gain: float32 [1600], replicated
The draws below stay inside these ranges and needn't reach their ends.
All inputs are finite; a program needn't handle non-finite values. No bound on the sum of `keep_mask` on one device may be relied on, other than what follows from the above.
Results may differ from the reference program's by a relative error of at most 0.02.
Values may be sent and summed in bfloat16 or wider, within the bound.
No kernel may reach another device: no remote copies, remote signals or barrier semaphores. Data moves between devices by JAX's collectives and lax.ppermute only.
A program may use at most 192 MiB of HBM per device.

```python
import math
import jax
import jax.numpy as jnp
from jax import lax

D = 1600
FF = 6400
TOK_DEV = 384
TOKENS = 12288
SAMPLES = 128


def draw_tokens(key, part):
    key_base, key_rows, key_cols = jax.random.split(key, 3)
    col_scale = jnp.exp(jax.random.uniform(key_cols, (1, D), jnp.float32, 0.0, math.log(10.0)))
    base = jnp.clip(jax.random.normal(key_base, (TOKENS, D), jnp.float32), -4.0, 4.0)
    row_scale = jnp.exp(jax.random.uniform(key_rows, (TOKENS, 1), jnp.float32, math.log(0.1), 0.0))
    return (base * row_scale * col_scale).astype(jnp.bfloat16)


def set_ends(entries, key, low, high):
    place = [jax.random.randint(jax.random.fold_in(key, axis), (), 0, length) for axis, length in enumerate(entries.shape)]
    longest = entries.shape.index(max(entries.shape))
    neighbour = place[:longest] + [(place[longest] + 1) % entries.shape[longest]] + place[longest + 1:]
    return entries.at[tuple(place)].set(low).at[tuple(neighbour)].set(high)


def spiked(values, rng, source, target, blocks, factor):
    def block_of(position):
        return (jnp.arange(values.shape[position]) // (values.shape[position] // blocks)).reshape((-1,) + (1,) * (values.ndim - 1 - position))

    near = jax.random.permutation(rng, blocks)[block_of(target)]
    far = (block_of(target) + blocks // 2) % blocks
    return jnp.where((block_of(source) == near) | (block_of(source) == far), factor * values, values)


def level_of(key, extent, cuts, smallest, top_value):
    def one(dim, parts):
        heights = jax.random.uniform(jax.random.fold_in(jax.random.fold_in(key, 6), dim), (parts,), jnp.float32, smallest / len(cuts), top_value / len(cuts))
        return jnp.repeat(jnp.exp(heights), extent[dim] // parts).reshape((-1,) + (1,) * (len(extent) - dim - 1))

    gain = one(*cuts[0])
    for cut in cuts[1:]:
        gain = gain * one(*cut)
    return gain


def centred(rng, shape, scale, reach, shards=(), dtype=jnp.bfloat16):
    array = jax.random.normal(rng, shape, jnp.float32) * scale
    if len(shards) > 0:
        array = level_of(rng, shape, shards, -0.22, 0.18) * array
    return jnp.clip(array, min=-reach, max=reach).astype(dtype)


def noise_with(key, shape, scale, most, pieces, heavy, held_as=jnp.bfloat16):
    array = scale * jax.random.normal(key, shape, jnp.float32)
    if pieces:
        array = array * level_of(key, shape, pieces, -0.22, 0.18)
    return jnp.clip(spiked(array, jax.random.fold_in(key, 3), *heavy), -most, most).astype(held_as)


def setup_inputs(seed: int = 0) -> dict:
    key_list = jax.random.split(jax.random.key(seed), 7)
    return {
        "tokens": draw_tokens(jax.random.fold_in(key_list[6], 71), 0),
        "norm_gain": jnp.clip(1.0 + 0.18 * jax.random.normal(key_list[1], (D,), jnp.float32), 0.1, 1.9),
        "up_weight": centred(key_list[2], (FF, D), D ** -0.5, 0.15625, ((0, 8),)),
        "up_bias": centred(key_list[3], (FF,), 0.5, 3.0, ((0, 8),)),
        "keep_mask": set_ends((jax.random.randint(key_list[4], (SAMPLES,), 0, 4) < 3).astype(jnp.int32), jax.random.fold_in(key_list[4], 1), 0, 1),
        "cotangent": noise_with(key_list[5], (TOKENS, FF), 1.0, 6.0, ((0, 32),), (0, 1, 32, 2.75)),
    }


def normalize(tokens, norm_gain):
    values = tokens.astype(jnp.float32)
    mean_sq = lax.optimization_barrier(jnp.mean(values * values, axis=1, keepdims=True))
    inv_rms = lax.rsqrt(mean_sq + 1e-06)
    x_hat = values * inv_rms
    return (x_hat, inv_rms, (x_hat * norm_gain[None, :]).astype(jnp.bfloat16))

def activate(preact):
    cdf = 0.5 * (1.0 + jax.scipy.special.erf(preact * 0.7071067811865476))
    density = jnp.exp(-0.5 * preact * preact) * 0.3989422804014327
    return (preact * cdf, cdf + preact * density)

def row_scales(keep_mask, total_rows):
    per_sample = keep_mask.astype(jnp.float32) * (4.0 / 3.0)
    return jnp.repeat(per_sample, total_rows // keep_mask.shape[0])

def reference(tokens, norm_gain, up_weight, up_bias, keep_mask, cotangent):
    x_hat, inv_rms, normed = normalize(tokens, norm_gain)
    preact = jnp.dot(normed, up_weight.T, preferred_element_type=jnp.float32) + up_bias.astype(jnp.float32)[None, :]
    gelu_out, slopes = activate(preact)
    scales = row_scales(keep_mask, tokens.shape[0])[:, None]
    hidden = (gelu_out * scales).astype(jnp.bfloat16)
    grad_pre = cotangent.astype(jnp.float32) * scales * slopes
    grad_low = grad_pre.astype(jnp.bfloat16)
    blocks = tokens.shape[0] // TOK_DEV
    grad_blocks = grad_low.reshape(blocks, TOK_DEV, FF)
    norm_blocks = normed.reshape(blocks, TOK_DEV, D)

    def add_block(total, pair):
        grad_part, norm_part = pair
        term = jnp.dot(grad_part.T, norm_part, preferred_element_type=jnp.float32).astype(jnp.bfloat16)
        term = lax.optimization_barrier(term)
        return (total + term.astype(jnp.float32), None)
    weight_sum = lax.scan(add_block, jnp.zeros((FF, D), jnp.float32), (grad_blocks, norm_blocks))[0]
    inv_root = 1.0 / math.sqrt(TOKENS)
    grad_norm = jnp.dot(grad_low, up_weight, preferred_element_type=jnp.float32)
    scaled = grad_norm * norm_gain[None, :]
    grad_in = (inv_rms * (scaled - x_hat * lax.optimization_barrier(jnp.mean(scaled * x_hat, axis=1, keepdims=True)))).astype(jnp.bfloat16)
    grad_gain = lax.optimization_barrier(jnp.sum(grad_norm * x_hat, axis=0)) * inv_root
    grad_bias = lax.optimization_barrier(jnp.sum(grad_pre, axis=0)) * inv_root
    return (hidden, grad_in, weight_sum * inv_root, grad_bias, grad_gain)
```

```python
import functools
import math

import jax
import jax.numpy as jnp
from jax import lax
from jax.experimental import pallas as pl
from jax.experimental.pallas import tpu as pltpu
from jax.sharding import PartitionSpec as P

CHUNKS = (160, 160, 160, 160, 160)
ORDER = (
    "O B0 B1 B3 ",
    "W0 R0 W2 B2 ",
    "W1 R1 S0 G ",
    "T0 S1 B4 W3 ",
    "T1 R2 W4 U0 ",
    "R3 S2 G U1 ",
    "S3 T2 R4 T3 ",
    "U2 S4 T4 H ",
    "U3 U4 ",
)


def normalize(tokens, norm_gain):
    values = tokens.astype(jnp.float32)
    mean_sq = jnp.mean(values * values, axis=1, keepdims=True)
    inv_rms = lax.rsqrt(mean_sq + 1e-06)
    x_hat = values * inv_rms
    return (x_hat, inv_rms, (x_hat * norm_gain[None, :]).astype(jnp.bfloat16))


def activate(preact):
    cdf = 0.5 * (1.0 + jax.scipy.special.erf(preact * 0.7071067811865476))
    density = jnp.exp(-0.5 * preact * preact) * 0.3989422804014327
    return (preact * cdf, cdf + preact * density)


def row_scales(keep_mask, total_rows):
    per_sample = keep_mask.astype(jnp.float32) * (4.0 / 3.0)
    return jnp.repeat(per_sample, total_rows // keep_mask.shape[0])


def contract_last(left, right):
    return lax.dot_general(
        left, right, (((1,), (1,)), ((), ())), preferred_element_type=jnp.float32
    )


def swap(value, bit):
    return lax.ppermute(value, "fsdp", [(i, i ^ bit) for i in range(8)])


def swap_core(value):
    return swap(value, 1)


def swap_x(value):
    return swap(value, 2)


def swap_y(value):
    return swap(value, 4)


LANES = 128


def work_body(sizes, spots, width, *refs):
    m = len(sizes)
    place, normed_hbm, flipped_hbm, scale = refs[:4]
    piece_hbm = refs[4 : 4 + m]
    outs = refs[4 + m + 3 :]
    states, low_hbm, grad_hbm = outs[:2], outs[3 : 3 + m], outs[3 + m : 3 + 2 * m]
    normed, flipped, pre, cot, hid = outs[3 + 2 * m : 8 + 2 * m]
    piece_v, low_v, grad_v = outs[8 + 2 * m : 11 + 2 * m]
    main_sem, in_sem, cot_sem, out_sem = outs[11 + 2 * m :]
    rows2 = normed.shape[0]
    rows = rows2 // 2
    depth = normed.shape[1]
    block = depth // 4
    begin = [sum(sizes[:j]) for j in range(m)]

    def near(j):
        return pl.ds(begin[j], sizes[j])

    def spot(j):
        start, side = spots[j]
        return pl.ds(pl.multiple_of(start + width * (place[0] ^ side), 16), sizes[j])

    copy = pltpu.make_async_copy
    flipped_in = [
        copy(flipped_hbm.at[pl.ds(i * block, block)], flipped.at[pl.ds(i * block, block)], main_sem.at[i])
        for i in range(4)
    ]
    part = rows2 // 4
    normed_in = [
        copy(normed_hbm.at[pl.ds(i * part, part)], normed.at[pl.ds(i * part, part)], main_sem.at[4 + i])
        for i in range(4)
    ]
    piece_in = [copy(piece_hbm[j], piece_v.at[near(j)], in_sem.at[j]) for j in range(m)]
    cot_in = [
        copy(states[i].at[spot(j)], cot.at[near(j), pl.ds(i * rows, rows)], cot_sem.at[2 * j + i])
        for j in range(m)
        for i in range(2)
    ]
    hid_out = [
        copy(hid.at[near(j), pl.ds(i * rows, rows)], states[i].at[spot(j)], out_sem.at[4 * j + i])
        for j in range(m)
        for i in range(2)
    ]
    low_out = [copy(low_v.at[near(j)], low_hbm[j], out_sem.at[4 * j + 2]) for j in range(m)]
    grad_out = [copy(grad_v.at[near(j)], grad_hbm[j], out_sem.at[4 * j + 3]) for j in range(m)]

    piece_in[0].start()
    for one in flipped_in:
        one.start()
    for one in cot_in[:2]:
        one.start()
    for one in normed_in:
        one.start()
    for j in range(1, m):
        piece_in[j].start()
        for one in cot_in[2 * j : 2 * j + 2]:
            one.start()
    for j in range(m):
        size = sizes[j]
        piece_in[j].wait()
        if j == 0:
            for one in flipped_in:
                one.wait()
        pre[:size, :] = jnp.dot(piece_v[near(j), :], flipped[...], preferred_element_type=jnp.float32)
        for one in cot_in[2 * j : 2 * j + 2]:
            one.wait()

        @pl.loop(0, size // 16)
        def _(strip):
            here = pl.ds(pl.multiple_of(strip * 16, 16), 16)
            there = pl.ds(pl.multiple_of(begin[j] + strip * 16, 16), 16)
            for col in range(0, rows2, 2 * LANES):
                cols = pl.ds(col, 2 * LANES)
                gelu_out, slopes = activate(pre[here, cols])
                factor = scale[:, cols]
                hid[there, cols] = (gelu_out * factor).astype(jnp.bfloat16)
                grad = cot[there, cols].astype(jnp.float32) * factor * slopes
                low_v[there, cols] = grad.astype(jnp.bfloat16)

        for one in hid_out[2 * j : 2 * j + 2]:
            one.start()
        low_out[j].start()
        if j == 0:
            for one in normed_in:
                one.wait()
        for col in range(0, depth, 4 * LANES):
            cols = pl.ds(col, min(4 * LANES, depth - col))
            grad_v[near(j), cols] = jnp.dot(
                low_v[near(j), :], normed[:, cols], preferred_element_type=jnp.float32
            ).astype(jnp.bfloat16)
        grad_out[j].start()
    for one in hid_out + low_out + grad_out:
        one.wait()


def call(body, operands, outs, aliases, scratch=(), limit=40):
    spec = {
        "hbm": pl.BlockSpec(memory_space=pltpu.HBM),
        "vmem": pl.BlockSpec(memory_space=pltpu.VMEM),
        "smem": pl.BlockSpec(memory_space=pltpu.SMEM),
    }
    return pl.pallas_call(
        body,
        out_shape=[jax.ShapeDtypeStruct(shape, dtype) for _, shape, dtype in outs],
        in_specs=[spec[space] for space, _ in operands],
        out_specs=[spec[space] for space, _, _ in outs],
        scratch_shapes=list(scratch),
        input_output_aliases=aliases,
        compiler_params=pltpu.CompilerParams(vmem_limit_bytes=limit * 1024 * 1024),
        cost_estimate=pl.CostEstimate(flops=0, bytes_accessed=0, transcendentals=0),
    )(*[value for _, value in operands])


def work(pieces, spots, width, place, normed, flipped, scale, states, token):
    sizes = [piece.shape[0] for piece in pieces]
    m, total = len(sizes), sum(sizes)
    rows2, depth = normed.shape
    low = jnp.bfloat16
    results = call(
        functools.partial(work_body, sizes, spots, width),
        [("smem", place), ("hbm", normed), ("hbm", flipped), ("vmem", scale)]
        + [("hbm", piece) for piece in pieces]
        + [("hbm", states[0]), ("hbm", states[1]), ("hbm", token)],
        [("hbm", states[0].shape, low), ("hbm", states[1].shape, low)]
        + [("hbm", token.shape, token.dtype)]
        + [("hbm", (size, rows2), low) for size in sizes]
        + [("hbm", (size, depth), low) for size in sizes],
        {4 + m: 0, 5 + m: 1, 6 + m: 2},
        [
            pltpu.VMEM((rows2, depth), low),
            pltpu.VMEM((depth, rows2), low),
            pltpu.VMEM((max(sizes), rows2), jnp.float32),
            pltpu.VMEM((total, rows2), low),
            pltpu.VMEM((total, rows2), low),
            pltpu.VMEM((total, depth), low),
            pltpu.VMEM((total, rows2), low),
            pltpu.VMEM((total, depth), low),
            pltpu.SemaphoreType.DMA((8,)),
            pltpu.SemaphoreType.DMA((m,)),
            pltpu.SemaphoreType.DMA((2 * m,)),
            pltpu.SemaphoreType.DMA((4 * m,)),
        ],
    )
    return results[:2], results[2], results[3 : 3 + m], results[3 + m :]


def total_body(count, extra, start, scale, *refs):
    terms = refs[:count]
    outs = refs[-6:-4] if scale else refs[-4:-3]
    values, result, sem = refs[-3:]
    ending = refs[-4]
    size, depth = terms[0].shape
    wide = result.shape[1]
    moves = [
        pltpu.make_async_copy(terms[i], values.at[i], sem.at[i]) for i in range(count)
    ]
    for one in moves:
        one.start()
    for one in moves:
        one.wait()

    @pl.loop(0, size // 16)
    def _(strip):
        here = pl.ds(pl.multiple_of(strip * 16, 16), 16)
        total = values[0, here, :].astype(jnp.float32)
        for i in range(1, count):
            total = total + values[i, here, :].astype(jnp.float32)
        if scale:
            total = total.astype(jnp.bfloat16).astype(jnp.float32) * scale
            ending[here, :] = total[:, depth - LANES :]
            total = total[:, :wide]
        result[here, :] = total.astype(result.dtype)

    if extra:
        tail = pl.ds(depth - LANES, LANES)
        result[:, tail] = (result[:, tail].astype(jnp.float32) + refs[count][...]).astype(result.dtype)
    if scale:
        here = pl.ds(start, size)
        back = [
            pltpu.make_async_copy(result, outs[0].at[here], sem.at[0]),
            pltpu.make_async_copy(ending, outs[1].at[here], sem.at[1]),
        ]
    else:
        back = [pltpu.make_async_copy(result, outs[0], sem.at[0])]
    for one in back:
        one.start()
    for one in back:
        one.wait()


def total_of(operands, token, extra=None):
    shape = operands[0].shape
    given = [("hbm", value) for value in operands]
    if extra is not None:
        given.append(("vmem", extra))
    results = call(
        functools.partial(total_body, len(operands), extra is not None, 0, None),
        given + [("hbm", token)],
        [("hbm", token.shape, token.dtype), ("hbm", shape, jnp.bfloat16)],
        {len(given): 0},
        [
            pltpu.VMEM((len(operands),) + shape, jnp.bfloat16),
            pltpu.VMEM(shape, jnp.bfloat16),
            pltpu.SemaphoreType.DMA((len(operands),)),
        ],
        limit=16,
    )
    return results[1], results[0]


def finish_of(operands, results, shapes, start, scale, token, before):
    shape = operands[0].shape
    given = [("hbm", value) for value in operands] + [("hbm", value) for value in before]
    aliases = {len(given): 0}
    given.append(("hbm", token))
    for i, value in enumerate(results):
        aliases[len(given)] = 1 + i
        given.append(("hbm", value))
    outs = call(
        functools.partial(total_body, len(operands), False, start, scale),
        given,
        [("hbm", token.shape, token.dtype)] + [("hbm", one, jnp.float32) for one in shapes],
        aliases,
        [
            pltpu.VMEM((shape[0], LANES), jnp.float32),
            pltpu.VMEM((len(operands),) + shape, jnp.bfloat16),
            pltpu.VMEM((shape[0], shapes[0][1]), jnp.float32),
            pltpu.SemaphoreType.DMA((len(operands),)),
        ],
        limit=16,
    )
    return outs[1:], outs[0]


def spread_body(sizes, more, last, *refs):
    m = len(sizes)
    low_hbm, piece_hbm = refs[:m], refs[m : 2 * m]
    acc, low_v, piece_v, sem = refs[-4:]
    begin = [sum(sizes[:j]) for j in range(m)]
    copy = pltpu.make_async_copy
    moves = []
    for j in range(m):
        here = pl.ds(begin[j], sizes[j])
        moves.append(copy(low_hbm[j], low_v.at[here], sem.at[2 * j]))
        moves.append(copy(piece_hbm[j], piece_v.at[here], sem.at[2 * j + 1]))
    if more:
        fetch = copy(refs[2 * m], acc, sem.at[2 * m])
        fetch.start()
    for one in moves:
        one.start()
    width = acc.shape[1]
    for group in range(0, m, 4):
        for one in moves[2 * group : 2 * group + 8]:
            one.wait()
        end = min(group + 4, m) - 1
        here = pl.ds(begin[group], begin[end] + sizes[end] - begin[group])
        turned = low_v[here, :].T
        if more and not group:
            fetch.wait()
        for col in range(0, width, 4 * LANES):
            cols = pl.ds(col, min(4 * LANES, width - col))
            part = jnp.dot(turned, piece_v[here, cols], preferred_element_type=jnp.float32)
            if group or more:
                part = part + acc[:, cols]
            acc[:, cols] = part
    if not last:
        out = copy(acc, refs[-5], sem.at[0])
        out.start()
        out.wait()
        return
    tokens, token_out, gain = refs[2 * m + more : 2 * m + more + 2], refs[-8], refs[-5]
    own, peer = refs[-7:-5]
    rows, depth = tokens[0].shape
    out = [
        copy(acc.at[pl.ds(0, rows)], own, sem.at[0]),
        copy(acc.at[pl.ds(rows, rows)], peer, sem.at[1]),
    ]
    for one in out:
        one.start()
    gain[...] = jnp.zeros_like(gain)
    for index, source in enumerate(tokens):

        @pl.loop(0, rows // 16)
        def _(strip):
            values = source[pl.ds(pl.multiple_of(strip * 16, 16), 16), :].astype(jnp.float32)
            x_hat = values * lax.rsqrt(jnp.mean(values * values, axis=1, keepdims=True) + 1e-06)
            here = pl.ds(pl.multiple_of(index * rows + strip * 16, 16), 16)
            product = acc[here, :depth] * x_hat
            gain[...] += product[:8] + product[8:]

    for one in out:
        one.wait()


def spread(lows, pieces, token, former=None, tokens=None):
    sizes = [low.shape[0] for low in lows]
    m, total = len(sizes), sum(sizes)
    rows2, depth = lows[0].shape[1], pieces[0].shape[1]
    given = [("hbm", low) for low in lows] + [("hbm", piece) for piece in pieces]
    if former is not None:
        given.append(("hbm", former))
    outs = [("hbm", token.shape, token.dtype)]
    if tokens is None:
        outs.append(("hbm", (rows2, depth), jnp.float32))
    else:
        given += [("vmem", one) for one in tokens]
        rows, narrow = tokens[0].shape
        outs += [("hbm", (rows, depth), jnp.float32)] * 2 + [("vmem", (8, narrow), jnp.float32)]
    results = call(
        functools.partial(spread_body, sizes, int(former is not None), tokens is not None),
        given + [("hbm", token)],
        outs,
        {len(given): 0},
        [
            pltpu.VMEM((rows2, depth), jnp.float32),
            pltpu.VMEM((total, rows2), jnp.bfloat16),
            pltpu.VMEM((total, depth), jnp.bfloat16),
            pltpu.SemaphoreType.DMA((2 * m + 1,)),
        ],
        limit=48,
    )
    return results[1:], results[0]


def pack_body(sizes, weight, bias, token, token_out, *outs):
    depth = weight.shape[1]
    full = outs[0].shape[1]
    lane = lax.broadcasted_iota(jnp.int32, (16, LANES), 1) + (full - LANES)
    start = 0
    for size, out in zip(sizes, outs):
        out[:, :depth] = weight[pl.ds(start, size), :]
        for row in range(0, size, 16):
            column = jnp.broadcast_to(bias[:, start + row : start + row + 16], (LANES, 16)).T
            last = out[row : row + 16, full - LANES :].astype(jnp.float32)
            last = jnp.where(lane < depth, last, jnp.where(lane == depth, column, 0.0))
            out[row : row + 16, full - LANES :] = last.astype(jnp.bfloat16)
        start += size


def pack(weight, bias, token):
    depth = weight.shape[1]
    full = depth + -depth % LANES
    results = call(
        functools.partial(pack_body, CHUNKS),
        [("vmem", weight), ("vmem", bias.astype(jnp.float32)[None, :]), ("hbm", token)],
        [("hbm", token.shape, token.dtype)]
        + [("vmem", (size, full), jnp.bfloat16) for size in CHUNKS],
        {2: 0},
    )
    return results[1:], results[0]


def ranges(units, width):
    for first in range(0, units, LANES):
        at, cuts = first, []
        while at < min(first + LANES, units):
            stop = min(first + LANES, units, (at // width + 1) * width)
            cuts.append((at // width, at % width, at - first, stop - at))
            at = stop
        yield first, cuts


def turn_body(width, place, cot, token, token_out, own, peer):
    core = place[1]
    for first, cuts in ranges(cot.shape[1], width):
        block = cot[:, first : first + LANES].T
        for shard, offset, at, size in cuts:
            to = pl.ds((shard // 2) * width + offset, size)
            mine = core == shard % 2

            @pl.when(mine)
            def _():
                own[to, :] = block[at : at + size]

            @pl.when(jnp.logical_not(mine))
            def _():
                peer[to, :] = block[at : at + size]


def turn(cotangent, width, place, token):
    rows, units = cotangent.shape
    half = ("vmem", (units // 2, rows), jnp.bfloat16)
    results = call(
        functools.partial(turn_body, width),
        [("smem", place), ("vmem", cotangent), ("hbm", token)],
        [("hbm", token.shape, token.dtype), half, half],
        {2: 0},
    )
    return results[1], results[2], results[0]


def back_body(width, place, own, peer, token, token_out, out):
    core = place[1]
    for first, cuts in ranges(out.shape[1], width):
        blocks = []
        for shard, offset, at, size in cuts:
            to = pl.ds((shard // 2) * width + offset, size)
            blocks.append(jnp.where(core == shard % 2, own[to, :], peer[to, :]))
        block = blocks[0] if len(blocks) == 1 else jnp.concatenate(blocks, axis=0)
        out[:, first : first + LANES] = block.T


def back(own, peer, width, place, token):
    units, rows = 2 * own.shape[0], own.shape[1]
    results = call(
        functools.partial(back_body, width),
        [("smem", place), ("vmem", own), ("vmem", peer), ("hbm", token)],
        [("hbm", token.shape, token.dtype), ("vmem", (rows, units), jnp.bfloat16)],
        {3: 0},
    )
    return results[1], results[0]


def norm_body(own, peer, gain, token, token_out, normed, flipped):
    rows, depth = own.shape
    full = normed.shape[1]
    spare = full - depth // LANES * LANES
    lane = lax.broadcasted_iota(jnp.int32, (LANES, LANES), 1) + (full - LANES)
    for index, source in enumerate((own, peer)):

        @pl.loop(0, rows // LANES)
        def _(strip):
            values = source[pl.ds(pl.multiple_of(strip * LANES, LANES), LANES), :].astype(jnp.float32)
            mean_sq = jnp.mean(values * values, axis=1, keepdims=True)
            value = values * lax.rsqrt(mean_sq + 1e-06) * gain[...]
            to = pl.ds(pl.multiple_of(index * rows + strip * LANES, LANES), LANES)
            normed[to, :depth] = value.astype(jnp.bfloat16)
            last = normed[to, full - LANES :]
            last = jnp.where(lane < depth, last, jnp.where(lane == depth, 1.0, 0.0).astype(jnp.bfloat16))
            normed[to, full - LANES :] = last
            for col in range(0, full, LANES):
                flipped[col : col + LANES, to] = normed[to, col : col + LANES].T


def norm(tokens, peer, norm_gain, token):
    rows, depth = tokens.shape
    full = depth + -depth % LANES
    results = call(
        norm_body,
        [("vmem", tokens), ("vmem", peer), ("vmem", norm_gain[None, :]), ("hbm", token)],
        [
            ("hbm", token.shape, token.dtype),
            ("vmem", (2 * rows, full), jnp.bfloat16),
            ("vmem", (full, 2 * rows), jnp.bfloat16),
        ],
        {3: 0},
    )
    return results[1], results[2], results[0]


def swap_plane(value, bit=1):
    return lax.ppermute(value, "rep", [(i, i ^ bit) for i in range(4)])


def paired(tokens, norm_gain, up_weight, up_bias, keep_mask, cotangent):
    rows, depth = tokens.shape
    width = up_weight.shape[0]
    index = lax.axis_index("fsdp")
    place = jnp.stack([index >> 1, index & 1]).astype(jnp.int32)
    inv_root = 1.0 / math.sqrt(rows * 32)
    count = len(CHUNKS)
    starts = [sum(CHUNKS[:c]) for c in range(count)]
    spare = -depth % LANES

    token = jnp.zeros((8, LANES), jnp.float32)
    own, token = pack(up_weight, up_bias, token)
    from_x = [swap_x(piece) for piece in own]
    from_y = [swap_y(piece) for piece in own]
    from_d = [swap_x(from_y[c]) if c % 2 == 0 else swap_y(from_x[c]) for c in range(count)]

    tokens_peer = swap_core(tokens)
    scale_own = row_scales(keep_mask, rows)
    scale = jnp.concatenate([scale_own, swap_core(scale_own)])[None, :]
    cot_own, cot_peer, token = turn(cotangent, width, place, token)
    normed, flipped, token = norm(tokens, tokens_peer, norm_gain, token)
    states = [cot_own, swap_core(cot_peer)]

    pieces = {}
    for c in range(count):
        pieces["O", c], pieces["X", c], pieces["Y", c] = own[c], from_x[c], from_y[c]
        pieces["D", c] = from_d[c]
    side = {"O": 0, "X": 1, "Y": 2, "D": 3}
    lows, grads, sent_x, sent_y, relayed = {}, {}, {}, {}, {}
    summed, across, used, results, former = {}, {}, set(), (), None
    hidden = grad_in = None

    def run(keys):
        nonlocal states, token
        spots = [(starts[c], side[kind]) for kind, c in keys]
        states, token, low, grad = work(
            [pieces[key] for key in keys], spots, width, place, normed, flipped, scale, states, token
        )
        for key, one, other in zip(keys, low, grad):
            lows[key], grads[key] = one, other

    for task in "".join(ORDER).split():
        kind, c = task[0], int(task[1:] or 0)
        even = c % 2 == 0
        if kind == "W":
            run([("X", c), ("Y", c)])
            if even:
                sent_y[c] = swap_y(grads["Y", c])
            else:
                sent_x[c] = swap_x(grads["X", c])
        elif kind == "B":
            run([("D", c)])
            relayed[c] = swap_y(grads["D", c]) if even else swap_x(grads["D", c])
        elif kind == "O":
            run([("O", k) for k in range(count)])
        elif kind == "R":
            value, token = total_of([grads["X" if even else "Y", c], relayed[c]], token)
            if even:
                sent_x[c] = swap_x(value)
            else:
                sent_y[c] = swap_y(value)
        elif kind == "S":
            extra = None
            if c == count - 1:
                lanes = jnp.pad(gain.reshape(depth // 16, 16), ((0, CHUNKS[c] - depth // 16), (0, 0)))
                extra = jnp.pad(lanes, ((0, 0), (LANES - 16, 0)))
            summed[c], token = total_of([grads["O", c], sent_x[c], sent_y[c]], token, extra)
            across[c] = swap_plane(summed[c], 1)
        elif kind == "T":
            summed[c], token = total_of([summed[c], across[c]], token)
            across[c] = swap_plane(summed[c], 2)
        elif kind == "U":
            shapes = [(width, depth), (width, LANES)]
            before = () if hidden is None else (hidden, grad_in)
            results, token = finish_of(
                [summed[c], across[c]], results, shapes, starts[c], inv_root, token, before
            )
        elif kind == "G":
            keys = [key for key in lows if key not in used]
            used.update(keys)
            given = [lows[key] for key in keys], [pieces[key] for key in keys]
            if len(used) < 4 * count:
                (former,), token = spread(*given, token, former)
            else:
                (whole, peer, gain), token = spread(*given, token, former, (tokens, tokens_peer))
                peer = swap_core(peer)
                gain = jnp.sum(gain, axis=0)
                gain = gain + swap_core(gain)
                gain = gain + swap_x(gain)
                gain = gain + swap_y(gain)
        elif kind == "H":
            hidden, token = back(states[0], swap_core(states[1]), width, place, token)
            x_hat, inv_rms, _ = normalize(tokens, norm_gain)
            scaled = (whole + peer)[:, :depth] * norm_gain[None, :]
            grad_in = (
                inv_rms * (scaled - x_hat * jnp.mean(scaled * x_hat, axis=1, keepdims=True))
            ).astype(jnp.bfloat16)

    grad_weight, tail = results
    grad_bias = tail[:, LANES - spare]
    grad_gain = tail[starts[-1] : starts[-1] + depth // 16, LANES - 16 :].reshape(depth)
    return (hidden, grad_in, grad_weight, grad_bias, grad_gain)


def local(tokens, norm_gain, up_weight, up_bias, keep_mask, cotangent):
    x_hat, inv_rms, normed = normalize(tokens, norm_gain)
    rows = tokens.shape[0]
    width = up_weight.shape[0]
    tok_total = rows * lax.axis_size("fsdp") * lax.axis_size("rep")
    inv_root = 1.0 / math.sqrt(tok_total)
    weight_all, bias_all = (
        lax.all_gather(up_weight, "fsdp", axis=0, tiled=True),
        lax.all_gather(up_bias, "fsdp", axis=0, tiled=True),
    )
    scales = row_scales(keep_mask, rows)[:, None]
    preact = contract_last(normed, weight_all) + bias_all.astype(jnp.float32)[None, :]
    gelu_out, slopes = activate(preact)
    hidden = (gelu_out * scales).astype(jnp.bfloat16)
    grad_pre = cotangent.astype(jnp.float32) * scales * slopes
    grad_low = grad_pre.astype(jnp.bfloat16)
    weight_part = lax.psum_scatter(
        lax.dot_general(
            grad_low, normed, (((0,), (0,)), ((), ())), preferred_element_type=jnp.float32
        ).astype(jnp.bfloat16),
        "fsdp",
        scatter_dimension=0,
        tiled=True,
    )
    weight_sum = lax.psum(weight_part, "rep").astype(jnp.float32)
    grad_norm = jnp.dot(grad_low, weight_all, preferred_element_type=jnp.float32)
    bias_total, gain_total = lax.psum(
        (jnp.sum(grad_pre, axis=0), jnp.sum(grad_norm * x_hat, axis=0)), ("fsdp", "rep")
    )
    bias_sum = lax.dynamic_slice_in_dim(bias_total, lax.axis_index("fsdp") * width, width, 0)
    scaled = grad_norm * norm_gain[None, :]
    grad_in = (inv_rms * (scaled - x_hat * jnp.mean(scaled * x_hat, axis=1, keepdims=True))).astype(
        jnp.bfloat16
    )
    return (hidden, grad_in, weight_sum * inv_root, bias_sum * inv_root, gain_total * inv_root)


def solution(mesh):
    body = paired if (mesh.shape["fsdp"], mesh.shape["rep"]) == (8, 4) else local
    return jax.shard_map(
        body,
        mesh=mesh,
        in_specs=(
            P(("fsdp", "rep"), None),
            P(),
            P("fsdp", None),
            P("fsdp"),
            P(("fsdp", "rep")),
            P(("fsdp", "rep"), None),
        ),
        out_specs=(
            P(("fsdp", "rep"), None),
            P(("fsdp", "rep"), None),
            P("fsdp", None),
            P("fsdp"),
            P(),
        ),
        check_vma=False,
    )
```

```python
import functools
import math

import jax
import jax.numpy as jnp
from jax import lax
from jax.experimental import pallas as pl
from jax.experimental.pallas import tpu as pltpu
from jax.sharding import PartitionSpec as P

CHUNKS = (192, 192, 160, 160, 96)
ORDER = (
    "W0 W1 B0 B1 ",
    "W3 B2 R0 R1 ",
    "O S0 S1 T0 ",
    "W4 B3 W2 V0 ",
    "T1 R2 B4 R3 ",
    "U0 G S2 V1 ",
    "R4 T2 ga S3 ",
    "U1 gb V2 gd ",
    "T3 S4 K U2 ",
    "T4 V3 H J ",
    "V4 U3 U4 ",
)


def normalize(tokens, norm_gain):
    values = tokens.astype(jnp.float32)
    mean_sq = jnp.mean(values * values, axis=1, keepdims=True)
    inv_rms = lax.rsqrt(mean_sq + 1e-06)
    x_hat = values * inv_rms
    return (x_hat, inv_rms, (x_hat * norm_gain[None, :]).astype(jnp.bfloat16))


def activate(preact):
    cdf = 0.5 * (1.0 + jax.scipy.special.erf(preact * 0.7071067811865476))
    density = jnp.exp(-0.5 * preact * preact) * 0.3989422804014327
    return (preact * cdf, cdf + preact * density)


def row_scales(keep_mask, total_rows):
    per_sample = keep_mask.astype(jnp.float32) * (4.0 / 3.0)
    return jnp.repeat(per_sample, total_rows // keep_mask.shape[0])


def contract_last(left, right):
    return lax.dot_general(
        left, right, (((1,), (1,)), ((), ())), preferred_element_type=jnp.float32
    )


def swap(value, bit):
    return lax.ppermute(value, "fsdp", [(i, i ^ bit) for i in range(8)])


def swap_core(value):
    return swap(value, 1)


def swap_x(value):
    return swap(value, 2)


def swap_y(value):
    return swap(value, 4)


LANES = 128


def work_body(sizes, spots, width, first, *refs):
    m = len(sizes)
    place, normed, flipped, scale = refs[:4]
    piece_hbm = refs[4 : 4 + m]
    outs = refs[4 + m + 3 + (not first) :]
    former = None if first else refs[4 + m + 3]
    states, acc, grad_hbm = outs[:2], outs[3], outs[4 : 4 + m]
    pre, cot, hid, piece_v, low_v, grad_v, in_sem, cot_sem, out_sem = outs[4 + m :]
    rows2 = normed.shape[0]
    rows = rows2 // 2
    depth = normed.shape[1]
    begin = [sum(sizes[:j]) for j in range(m)]

    def near(j):
        return pl.ds(begin[j], sizes[j])

    def spot(j):
        start, side = spots[j]
        return pl.ds(pl.multiple_of(start + width * (place[0] ^ side), 16), sizes[j])

    copy = pltpu.make_async_copy
    piece_in = [copy(piece_hbm[j], piece_v.at[near(j)], in_sem.at[j]) for j in range(m)]
    cot_in = [
        copy(states[i].at[spot(j)], cot.at[near(j), pl.ds(i * rows, rows)], cot_sem.at[2 * j + i])
        for j in range(m)
        for i in range(2)
    ]
    hid_out = [
        copy(hid.at[near(j), pl.ds(i * rows, rows)], states[i].at[spot(j)], out_sem.at[3 * j + i])
        for j in range(m)
        for i in range(2)
    ]
    grad_out = [copy(grad_v.at[near(j)], grad_hbm[j], out_sem.at[3 * j + 2]) for j in range(m)]

    for j in range(m):
        piece_in[j].start()
        for one in cot_in[2 * j : 2 * j + 2]:
            one.start()
    for j in range(m):
        size = sizes[j]
        piece_in[j].wait()
        pre[:size, :] = jnp.dot(piece_v[near(j), :], flipped[...], preferred_element_type=jnp.float32)
        for one in cot_in[2 * j : 2 * j + 2]:
            one.wait()

        @pl.loop(0, size // 16)
        def _(strip):
            here = pl.ds(pl.multiple_of(strip * 16, 16), 16)
            there = pl.ds(pl.multiple_of(begin[j] + strip * 16, 16), 16)
            for col in range(0, rows2, 2 * LANES):
                cols = pl.ds(col, 2 * LANES)
                gelu_out, slopes = activate(pre[here, cols])
                factor = scale[:, cols]
                hid[there, cols] = (gelu_out * factor).astype(jnp.bfloat16)
                grad = cot[there, cols].astype(jnp.float32) * factor * slopes
                low_v[there, cols] = grad.astype(jnp.bfloat16)

        for one in hid_out[2 * j : 2 * j + 2]:
            one.start()
        for col in range(0, depth, 4 * LANES):
            cols = pl.ds(col, min(4 * LANES, depth - col))
            grad_v[near(j), cols] = jnp.dot(
                low_v[near(j), :], normed[:, cols], preferred_element_type=jnp.float32
            ).astype(jnp.bfloat16)
        grad_out[j].start()
    turned = low_v[...].T
    for col in range(0, depth, 4 * LANES):
        cols = pl.ds(col, min(4 * LANES, depth - col))
        part = jnp.dot(turned, piece_v[:, cols], preferred_element_type=jnp.float32)
        acc[:, cols] = part if first else former[:, cols] + part
    for one in hid_out + grad_out:
        one.wait()


def call(body, operands, outs, aliases, scratch=(), limit=16):
    spec = {
        "hbm": pl.BlockSpec(memory_space=pltpu.HBM),
        "vmem": pl.BlockSpec(memory_space=pltpu.VMEM),
        "smem": pl.BlockSpec(memory_space=pltpu.SMEM),
    }
    return pl.pallas_call(
        body,
        out_shape=[jax.ShapeDtypeStruct(shape, dtype) for _, shape, dtype in outs],
        in_specs=[spec[space] for space, _ in operands],
        out_specs=[spec[space] for space, _, _ in outs],
        scratch_shapes=list(scratch),
        input_output_aliases=aliases,
        compiler_params=pltpu.CompilerParams(vmem_limit_bytes=limit * 1024 * 1024),
        cost_estimate=pl.CostEstimate(flops=0, bytes_accessed=0, transcendentals=0),
    )(*[value for _, value in operands])


def work(pieces, spots, width, place, normed, flipped, scale, states, token, acc):
    sizes = [piece.shape[0] for piece in pieces]
    m, total = len(sizes), sum(sizes)
    rows2, depth = normed.shape
    low = jnp.bfloat16
    first = acc is None
    results = call(
        functools.partial(work_body, sizes, spots, width, first),
        [("smem", place), ("vmem", normed), ("vmem", flipped), ("vmem", scale)]
        + [("hbm", piece) for piece in pieces]
        + [("hbm", states[0]), ("hbm", states[1]), ("hbm", token)]
        + ([] if first else [("vmem", acc)]),
        [("hbm", states[0].shape, low), ("hbm", states[1].shape, low)]
        + [("hbm", token.shape, token.dtype), ("vmem", (rows2, depth), jnp.float32)]
        + [("hbm", (size, depth), low) for size in sizes],
        {4 + m: 0, 5 + m: 1, 6 + m: 2} | ({} if first else {7 + m: 3}),
        [
            pltpu.VMEM((max(sizes), rows2), jnp.float32),
            pltpu.VMEM((total, rows2), low),
            pltpu.VMEM((total, rows2), low),
            pltpu.VMEM((total, depth), low),
            pltpu.VMEM((total, rows2), low),
            pltpu.VMEM((total, depth), low),
            pltpu.SemaphoreType.DMA((m,)),
            pltpu.SemaphoreType.DMA((2 * m,)),
            pltpu.SemaphoreType.DMA((3 * m,)),
        ],
        limit=26,
    )
    return results[:2], results[2], results[3], results[4:]


def tie(token, *done):
    return call(
        lambda *refs: None,
        [("hbm", value) for value in done] + [("hbm", token)],
        [("hbm", token.shape, token.dtype)],
        {len(done): 0},
        limit=4,
    )[0]


def total_body(count, halves, extra, *refs):
    place, terms = refs[0], refs[1 : 1 + count]
    values, result, sem = refs[-3:]
    outs = refs[-5:-3] if halves else refs[-4:-3]
    size, depth = terms[0].shape
    moves = [pltpu.make_async_copy(terms[i], values.at[i], sem.at[i]) for i in range(count)]
    for one in moves:
        one.start()
    for one in moves:
        one.wait()

    @pl.loop(0, size // 16)
    def _(strip):
        here = pl.ds(pl.multiple_of(strip * 16, 16), 16)
        total = values[0, here, :].astype(jnp.float32)
        for i in range(1, count):
            total = total + values[i, here, :].astype(jnp.float32)
        result[here, :] = total.astype(result.dtype)
        if extra:
            tail = pl.ds(depth - LANES, LANES)
            result[here, tail] = (total[:, depth - LANES :] + refs[1 + count][here, :]).astype(result.dtype)

    if halves:
        half = size // 2
        back = [
            pltpu.make_async_copy(
                result.at[pl.ds(pl.multiple_of((place[2] ^ i) * half, 16), half)], outs[i], sem.at[i]
            )
            for i in range(2)
        ]
    else:
        back = [pltpu.make_async_copy(result, outs[0], sem.at[0])]
    for one in back:
        one.start()
    for one in back:
        one.wait()


def total_of(operands, place, token, halves=False, extra=None):
    rows, depth = operands[0].shape
    given = [("smem", place)] + [("hbm", value) for value in operands]
    if extra is not None:
        given.append(("vmem", extra))
    outs = [("hbm", (rows // 2, depth), jnp.bfloat16)] * 2 if halves else [("hbm", (rows, depth), jnp.bfloat16)]
    results = call(
        functools.partial(total_body, len(operands), halves, extra is not None),
        given + [("hbm", token)],
        [("hbm", token.shape, token.dtype)] + outs,
        {len(given): 0},
        [
            pltpu.VMEM((len(operands), rows, depth), jnp.bfloat16),
            pltpu.VMEM((rows, depth), jnp.bfloat16),
            pltpu.SemaphoreType.DMA((len(operands),)),
        ],
        limit=8,
    )
    return (results[1:] if halves else results[1]), results[0]


def finish_body(start, scale, place, mine, other, *refs):
    outs = refs[-6:-4]
    ending, values, result, sem = refs[-4:]
    half, depth = mine.shape
    wide = result.shape[1]
    moves = [
        pltpu.make_async_copy(
            one, values.at[pl.ds(pl.multiple_of((place[2] ^ i) * half, 16), half)], sem.at[i]
        )
        for i, one in enumerate((mine, other))
    ]
    for one in moves:
        one.start()
    for one in moves:
        one.wait()

    @pl.loop(0, 2 * half // 16)
    def _(strip):
        here = pl.ds(pl.multiple_of(strip * 16, 16), 16)
        total = values[here, :].astype(jnp.float32) * scale
        ending[here, :] = total[:, depth - LANES :]
        result[here, :] = total[:, :wide]

    here = pl.ds(start, 2 * half)
    back = [
        pltpu.make_async_copy(result, outs[0].at[here], sem.at[0]),
        pltpu.make_async_copy(ending, outs[1].at[here], sem.at[1]),
    ]
    for one in back:
        one.start()
    for one in back:
        one.wait()


def finish_of(mine, other, results, shapes, start, scale, place, token):
    half, depth = mine.shape
    given = [("smem", place), ("hbm", mine), ("hbm", other)]
    aliases = {len(given): 0}
    given.append(("hbm", token))
    for i, value in enumerate(results):
        aliases[len(given)] = 1 + i
        given.append(("hbm", value))
    outs = call(
        functools.partial(finish_body, start, scale),
        given,
        [("hbm", token.shape, token.dtype)] + [("hbm", one, jnp.float32) for one in shapes],
        aliases,
        [
            pltpu.VMEM((2 * half, LANES), jnp.float32),
            pltpu.VMEM((2 * half, depth), jnp.bfloat16),
            pltpu.VMEM((2 * half, shapes[0][1]), jnp.float32),
            pltpu.SemaphoreType.DMA((2,)),
        ],
        limit=8,
    )
    return outs[1:], outs[0]


def gains_body(acc, plain, token, token_out, gain):
    rows2, depth = plain.shape
    gain[...] = jnp.zeros_like(gain)

    @pl.loop(0, rows2 // 16)
    def _(strip):
        here = pl.ds(pl.multiple_of(strip * 16, 16), 16)
        values = plain[here, :].astype(jnp.float32)
        x_hat = values * lax.rsqrt(jnp.mean(values * values, axis=1, keepdims=True) + 1e-06)
        product = acc[here, :depth] * x_hat
        gain[...] += product[:8] + product[8:]


def gains(acc, plain, token):
    results = call(
        gains_body,
        [("vmem", acc), ("vmem", plain), ("hbm", token)],
        [("hbm", token.shape, token.dtype), ("vmem", (8, plain.shape[1]), jnp.float32)],
        {2: 0},
    )
    return results[1], results[0]


def close_body(acc, state, token, token_out, state_out, own, peer, sem):
    rows = own.shape[0]
    out = [
        pltpu.make_async_copy(acc.at[pl.ds(0, rows)], own, sem.at[0]),
        pltpu.make_async_copy(acc.at[pl.ds(rows, rows)], peer, sem.at[1]),
    ]
    for one in out:
        one.start()
    for one in out:
        one.wait()


def close(acc, state, token):
    rows2, full = acc.shape
    half = ("hbm", (rows2 // 2, full), jnp.float32)
    results = call(
        close_body,
        [("vmem", acc), ("hbm", state), ("hbm", token)],
        [("hbm", token.shape, token.dtype), ("hbm", state.shape, state.dtype), half, half],
        {1: 1, 2: 0},
        [pltpu.SemaphoreType.DMA((2,))],
    )
    return results[1:], results[0]


def pack_body(sizes, weight, bias, token, token_out, *outs):
    depth = weight.shape[1]
    full = outs[0].shape[1]
    lane = lax.broadcasted_iota(jnp.int32, (16, LANES), 1) + (full - LANES)
    start = 0
    for size, out in zip(sizes, outs):
        out[:, :depth] = weight[pl.ds(start, size), :]
        for row in range(0, size, 16):
            column = jnp.broadcast_to(bias[:, start + row : start + row + 16], (LANES, 16)).T
            last = out[row : row + 16, full - LANES :].astype(jnp.float32)
            last = jnp.where(lane < depth, last, jnp.where(lane == depth, column, 0.0))
            out[row : row + 16, full - LANES :] = last.astype(jnp.bfloat16)
        start += size


def pack(weight, bias, token):
    depth = weight.shape[1]
    full = depth + -depth % LANES
    results = call(
        functools.partial(pack_body, CHUNKS),
        [("vmem", weight), ("vmem", bias.astype(jnp.float32)[None, :]), ("hbm", token)],
        [("hbm", token.shape, token.dtype)]
        + [("vmem", (size, full), jnp.bfloat16) for size in CHUNKS],
        {2: 0},
    )
    return results[1:], results[0]


def ranges(units, width):
    for first in range(0, units, LANES):
        at, cuts = first, []
        while at < min(first + LANES, units):
            stop = min(first + LANES, units, (at // width + 1) * width)
            cuts.append((at // width, at % width, at - first, stop - at))
            at = stop
        yield first, cuts


def turn_body(width, place, cot, cot_peer, token, token_out, own, peer):
    core = place[1]
    for source, out in ((cot, own), (cot_peer, peer)):
        for parity in range(2):

            @pl.when(core == parity)
            def _():
                for first, cuts in ranges(source.shape[1], width):
                    cuts = [cut for cut in cuts if cut[0] % 2 == parity]
                    if cuts:
                        block = source[:, first : first + LANES].T
                    for shard, offset, at, size in cuts:
                        to = pl.ds((shard // 2) * width + offset, size)
                        out[to, :] = block[at : at + size]


def turn(cotangent, cot_peer, width, place, token):
    rows, units = cotangent.shape
    half = ("vmem", (units // 2, rows), jnp.bfloat16)
    results = call(
        functools.partial(turn_body, width),
        [("smem", place), ("vmem", cotangent), ("vmem", cot_peer), ("hbm", token)],
        [("hbm", token.shape, token.dtype), half, half],
        {3: 0},
        limit=20,
    )
    return results[1:], results[0]


def back_body(width, place, own, peer, token, token_out, out):
    core = place[1]
    for first, cuts in ranges(out.shape[1], width):
        blocks = []
        for shard, offset, at, size in cuts:
            to = pl.ds((shard // 2) * width + offset, size)
            blocks.append(jnp.where(core == shard % 2, own[to, :], peer[to, :]))
        block = blocks[0] if len(blocks) == 1 else jnp.concatenate(blocks, axis=0)
        out[:, first : first + LANES] = block.T


def back(own, peer, width, place, token):
    units, rows = 2 * own.shape[0], own.shape[1]
    results = call(
        functools.partial(back_body, width),
        [("smem", place), ("vmem", own), ("vmem", peer), ("hbm", token)],
        [("hbm", token.shape, token.dtype), ("vmem", (rows, units), jnp.bfloat16)],
        {3: 0},
    )
    return results[1], results[0]


def norm_body(own, peer, gain, token, token_out, normed, flipped, plain):
    depth, rows = own.shape
    full = normed.shape[1]
    lane = lax.broadcasted_iota(jnp.int32, (LANES, LANES), 1) + (full - LANES)
    for index, source in enumerate((own, peer)):
        for strip in range(0, rows, LANES):
            to = pl.ds(index * rows + strip, LANES)
            for col in range(0, depth, LANES):
                wide = min(LANES, depth - col)
                plain[to, col : col + wide] = source[col : col + wide, strip : strip + LANES].T
            values = plain[to, :].astype(jnp.float32)
            mean_sq = jnp.mean(values * values, axis=1, keepdims=True)
            value = values * lax.rsqrt(mean_sq + 1e-06) * gain[...]
            normed[to, :depth] = value.astype(jnp.bfloat16)
            last = normed[to, full - LANES :]
            last = jnp.where(lane < depth, last, jnp.where(lane == depth, 1.0, 0.0).astype(jnp.bfloat16))
            normed[to, full - LANES :] = last
            for col in range(0, full, LANES):
                flipped[col : col + LANES, to] = normed[to, col : col + LANES].T


def norm(tokens, peer, norm_gain, token):
    depth, rows = tokens.shape
    full = depth + -depth % LANES
    results = call(
        norm_body,
        [("vmem", tokens), ("vmem", peer), ("vmem", norm_gain[None, :]), ("hbm", token)],
        [
            ("hbm", token.shape, token.dtype),
            ("vmem", (2 * rows, full), jnp.bfloat16),
            ("vmem", (full, 2 * rows), jnp.bfloat16),
            ("vmem", (2 * rows, depth), jnp.bfloat16),
        ],
        {3: 0},
        limit=16,
    )
    return results[1:], results[0]


def swap_plane(value, bit=1):
    return lax.ppermute(value, "rep", [(i, i ^ bit) for i in range(4)])


def paired(tokens, norm_gain, up_weight, up_bias, keep_mask, cotangent):
    rows, depth = tokens.shape
    width = up_weight.shape[0]
    index = lax.axis_index("fsdp")
    plane = lax.axis_index("rep")
    place = jnp.stack([index >> 1, index & 1, plane & 1]).astype(jnp.int32)
    inv_root = 1.0 / math.sqrt(rows * 32)
    count = len(CHUNKS)
    starts = [sum(CHUNKS[:c]) for c in range(count)]
    spare = -depth % LANES

    token = jnp.zeros((8, LANES), jnp.float32)
    own, token = pack(up_weight, up_bias, token)
    from_x = [swap_x(piece) for piece in own]
    from_y = [swap_y(piece) for piece in own]
    from_d = [swap_x(from_y[c]) if c % 2 == 0 else swap_y(from_x[c]) for c in range(count)]

    flat = tokens.T
    (normed, flipped, plain), token = norm(flat, swap_core(flat), norm_gain, token)
    scale_own = row_scales(keep_mask, rows)
    scale = jnp.concatenate([scale_own, swap_core(scale_own)])[None, :]
    states, token = turn(cotangent, swap_core(cotangent), width, place, token)

    pieces = {}
    for c in range(count):
        pieces["O", c], pieces["X", c], pieces["Y", c] = own[c], from_x[c], from_y[c]
        pieces["D", c] = from_d[c]
    side = {"O": 0, "X": 1, "Y": 2, "D": 3}
    grads, sent_x, sent_y, relayed = {}, {}, {}, {}
    kept, across, results, acc = {}, {}, (), None
    hidden = grad_in = None

    def run(keys):
        nonlocal states, token, acc
        spots = [(starts[c], side[kind]) for kind, c in keys]
        states, token, acc, grad = work(
            [pieces[key] for key in keys], spots, width, place, normed, flipped, scale, states, token, acc
        )
        grads.update(zip(keys, grad))

    for task in "".join(ORDER).split():
        kind, c = task[0], int(task[1:]) if task[1:].isdigit() else 0
        even = c % 2 == 0
        if kind == "W":
            run([("X", c), ("Y", c)])
            if even:
                sent_y[c] = swap_y(grads["Y", c])
            else:
                sent_x[c] = swap_x(grads["X", c])
        elif kind == "B":
            run([("D", c)])
            relayed[c] = swap_y(grads["D", c]) if even else swap_x(grads["D", c])
        elif kind == "O":
            run([("O", k) for k in range(count)])
        elif kind == "R":
            value, token = total_of([grads["X" if even else "Y", c], relayed[c]], place, token)
            if even:
                sent_x[c] = swap_x(value)
            else:
                sent_y[c] = swap_y(value)
        elif kind == "S":
            extra = None
            if c == count - 1:
                lanes = gain.reshape(depth // 32, 32)
                extra = jnp.pad(lanes, ((0, CHUNKS[c] - depth // 32), (LANES - 32, 0)))
            terms = [grads["O", c], sent_x[c], sent_y[c]]
            (kept[c], other), token = total_of(terms, place, token, True, extra)
            across[c] = swap_plane(other, 1)
        elif kind == "T":
            kept[c], token = total_of([kept[c], across[c]], place, token)
            across[c] = swap_plane(kept[c], 2)
        elif kind == "V":
            kept[c], token = total_of([kept[c], across[c]], place, token)
            across[c] = swap_plane(kept[c], 1)
        elif kind == "U":
            shapes = [(width, depth), (width, LANES)]
            results, token = finish_of(
                kept[c], across[c], results, shapes, starts[c], inv_root, place, token
            )
        elif kind == "G":
            gain, token = gains(acc, plain, token)
            gain = jnp.sum(gain, axis=0)
            gain = gain + swap_core(gain)
        elif kind == "g":
            token = tie(token, gain)
            if task == "ga":
                gain = gain + swap_x(gain)
            elif task == "gb":
                gain = gain + swap_y(gain)
        elif kind == "K":
            (state, whole, peer), token = close(acc, states[1], token)
            state, peer = swap_core(state), swap_core(peer)
        elif kind == "H":
            hidden, token = back(states[0], state, width, place, token)
        elif kind == "J":
            x_hat, inv_rms, _ = normalize(plain[:rows], norm_gain)
            scaled = (whole + peer)[:, :depth] * norm_gain[None, :]
            grad_in = (
                inv_rms * (scaled - x_hat * jnp.mean(scaled * x_hat, axis=1, keepdims=True))
            ).astype(jnp.bfloat16)
            token = tie(token, grad_in)

    grad_weight, tail = results
    grad_bias = tail[:, LANES - spare]
    grad_gain = tail[starts[-1] : starts[-1] + depth // 32, LANES - 32 :].reshape(depth)
    return (hidden, grad_in, grad_weight, grad_bias, grad_gain)


def local(tokens, norm_gain, up_weight, up_bias, keep_mask, cotangent):
    x_hat, inv_rms, normed = normalize(tokens, norm_gain)
    rows = tokens.shape[0]
    width = up_weight.shape[0]
    tok_total = rows * lax.axis_size("fsdp") * lax.axis_size("rep")
    inv_root = 1.0 / math.sqrt(tok_total)
    weight_all, bias_all = (
        lax.all_gather(up_weight, "fsdp", axis=0, tiled=True),
        lax.all_gather(up_bias, "fsdp", axis=0, tiled=True),
    )
    scales = row_scales(keep_mask, rows)[:, None]
    preact = contract_last(normed, weight_all) + bias_all.astype(jnp.float32)[None, :]
    gelu_out, slopes = activate(preact)
    hidden = (gelu_out * scales).astype(jnp.bfloat16)
    grad_pre = cotangent.astype(jnp.float32) * scales * slopes
    grad_low = grad_pre.astype(jnp.bfloat16)
    weight_part = lax.psum_scatter(
        lax.dot_general(
            grad_low, normed, (((0,), (0,)), ((), ())), preferred_element_type=jnp.float32
        ).astype(jnp.bfloat16),
        "fsdp",
        scatter_dimension=0,
        tiled=True,
    )
    weight_sum = lax.psum(weight_part, "rep").astype(jnp.float32)
    grad_norm = jnp.dot(grad_low, weight_all, preferred_element_type=jnp.float32)
    bias_total, gain_total = lax.psum(
        (jnp.sum(grad_pre, axis=0), jnp.sum(grad_norm * x_hat, axis=0)), ("fsdp", "rep")
    )
    bias_sum = lax.dynamic_slice_in_dim(bias_total, lax.axis_index("fsdp") * width, width, 0)
    scaled = grad_norm * norm_gain[None, :]
    grad_in = (inv_rms * (scaled - x_hat * jnp.mean(scaled * x_hat, axis=1, keepdims=True))).astype(
        jnp.bfloat16
    )
    return (hidden, grad_in, weight_sum * inv_root, bias_sum * inv_root, gain_total * inv_root)


def solution(mesh):
    body = paired if (mesh.shape["fsdp"], mesh.shape["rep"]) == (8, 4) else local
    return jax.shard_map(
        body,
        mesh=mesh,
        in_specs=(
            P(("fsdp", "rep"), None),
            P(),
            P("fsdp", None),
            P("fsdp"),
            P(("fsdp", "rep")),
            P(("fsdp", "rep"), None),
        ),
        out_specs=(
            P(("fsdp", "rep"), None),
            P(("fsdp", "rep"), None),
            P("fsdp", None),
            P("fsdp"),
            P(),
        ),
        check_vma=False,
    )
```

```python
import functools
import math

import jax
import jax.numpy as jnp
from jax import lax
from jax.experimental import pallas as pl
from jax.experimental.pallas import tpu as pltpu
from jax.sharding import PartitionSpec as P

CHUNKS = (192, 192, 160, 160, 96)
ORDER = (
    "Oa r0 W0 r1 ",
    "W1 B0 B1 W2 ",
    "B2 R0 R1 Ob ",
    "S0 S1 T0 W3 ",
    "B3 W4 V0 T1 ",
    "R2 B4 R3 U0 ",
    "G S2 V1 R4 ",
    "T2 ga S3 U1 ",
    "gb V2 gd T3 ",
    "S4 U2 T4 V3 ",
    "K V4 H J ",
    "U3 U4 ",
)


def normalize(tokens, norm_gain):
    values = tokens.astype(jnp.float32)
    mean_sq = jnp.mean(values * values, axis=1, keepdims=True)
    inv_rms = lax.rsqrt(mean_sq + 1e-06)
    x_hat = values * inv_rms
    return (x_hat, inv_rms, (x_hat * norm_gain[None, :]).astype(jnp.bfloat16))


def activate(preact):
    cdf = 0.5 * (1.0 + jax.scipy.special.erf(preact * 0.7071067811865476))
    density = jnp.exp(-0.5 * preact * preact) * 0.3989422804014327
    return (preact * cdf, cdf + preact * density)


def row_scales(keep_mask, total_rows):
    per_sample = keep_mask.astype(jnp.float32) * (4.0 / 3.0)
    return jnp.repeat(per_sample, total_rows // keep_mask.shape[0])


def contract_last(left, right):
    return lax.dot_general(
        left, right, (((1,), (1,)), ((), ())), preferred_element_type=jnp.float32
    )


def swap(value, bit):
    return lax.ppermute(value, "fsdp", [(i, i ^ bit) for i in range(8)])


def swap_core(value):
    return swap(value, 1)


def swap_x(value):
    return swap(value, 2)


def swap_y(value):
    return swap(value, 4)


LANES = 128


def work_body(sizes, spots, width, first, *refs):
    m = len(sizes)
    place, normed, flipped, scale = refs[:4]
    piece_hbm = refs[4 : 4 + m]
    outs = refs[4 + m + 3 + (not first) :]
    former = None if first else refs[4 + m + 3]
    states, acc, grad_hbm = outs[:2], outs[3], outs[4 : 4 + m]
    pre, cot, hid, piece_v, low_v, grad_v, in_sem, cot_sem, out_sem = outs[4 + m :]
    rows2 = normed.shape[0]
    rows = rows2 // 2
    depth = normed.shape[1]
    begin = [sum(sizes[:j]) for j in range(m)]

    def near(j):
        return pl.ds(begin[j], sizes[j])

    def spot(j):
        start, side = spots[j]
        return pl.ds(pl.multiple_of(start + width * (place[0] ^ side), 16), sizes[j])

    copy = pltpu.make_async_copy
    piece_in = [copy(piece_hbm[j], piece_v.at[near(j)], in_sem.at[j]) for j in range(m)]
    cot_in = [
        copy(states[i].at[spot(j)], cot.at[near(j), pl.ds(i * rows, rows)], cot_sem.at[2 * j + i])
        for j in range(m)
        for i in range(2)
    ]
    hid_out = [
        copy(hid.at[near(j), pl.ds(i * rows, rows)], states[i].at[spot(j)], out_sem.at[3 * j + i])
        for j in range(m)
        for i in range(2)
    ]
    grad_out = [copy(grad_v.at[near(j)], grad_hbm[j], out_sem.at[3 * j + 2]) for j in range(m)]

    for j in range(m):
        piece_in[j].start()
        for one in cot_in[2 * j : 2 * j + 2]:
            one.start()
    for j in range(m):
        size = sizes[j]
        piece_in[j].wait()
        pre[:size, :] = jnp.dot(piece_v[near(j), :], flipped[...], preferred_element_type=jnp.float32)
        for one in cot_in[2 * j : 2 * j + 2]:
            one.wait()

        @pl.loop(0, size // 16)
        def _(strip):
            here = pl.ds(pl.multiple_of(strip * 16, 16), 16)
            there = pl.ds(pl.multiple_of(begin[j] + strip * 16, 16), 16)
            for col in range(0, rows2, 2 * LANES):
                cols = pl.ds(col, 2 * LANES)
                gelu_out, slopes = activate(pre[here, cols])
                factor = scale[:, cols]
                hid[there, cols] = (gelu_out * factor).astype(jnp.bfloat16)
                grad = cot[there, cols].astype(jnp.float32) * factor * slopes
                low_v[there, cols] = grad.astype(jnp.bfloat16)

        for one in hid_out[2 * j : 2 * j + 2]:
            one.start()
        for col in range(0, depth, 4 * LANES):
            cols = pl.ds(col, min(4 * LANES, depth - col))
            grad_v[near(j), cols] = jnp.dot(
                low_v[near(j), :], normed[:, cols], preferred_element_type=jnp.float32
            ).astype(jnp.bfloat16)
        grad_out[j].start()
    turned = low_v[...].T
    for col in range(0, depth, 4 * LANES):
        cols = pl.ds(col, min(4 * LANES, depth - col))
        part = jnp.dot(turned, piece_v[:, cols], preferred_element_type=jnp.float32)
        acc[:, cols] = part if first else former[:, cols] + part
    for one in hid_out + grad_out:
        one.wait()


def call(body, operands, outs, aliases, scratch=(), limit=16):
    spec = {
        "hbm": pl.BlockSpec(memory_space=pltpu.HBM),
        "vmem": pl.BlockSpec(memory_space=pltpu.VMEM),
        "smem": pl.BlockSpec(memory_space=pltpu.SMEM),
    }
    return pl.pallas_call(
        body,
        out_shape=[jax.ShapeDtypeStruct(shape, dtype) for _, shape, dtype in outs],
        in_specs=[spec[space] for space, _ in operands],
        out_specs=[spec[space] for space, _, _ in outs],
        scratch_shapes=list(scratch),
        input_output_aliases=aliases,
        compiler_params=pltpu.CompilerParams(vmem_limit_bytes=limit * 1024 * 1024),
        cost_estimate=pl.CostEstimate(flops=0, bytes_accessed=0, transcendentals=0),
    )(*[value for _, value in operands])


def work(pieces, spots, width, place, normed, flipped, scale, states, token, acc):
    sizes = [piece.shape[0] for piece in pieces]
    m, total = len(sizes), sum(sizes)
    rows2, depth = normed.shape
    low = jnp.bfloat16
    first = acc is None
    results = call(
        functools.partial(work_body, sizes, spots, width, first),
        [("smem", place), ("vmem", normed), ("vmem", flipped), ("vmem", scale)]
        + [("hbm", piece) for piece in pieces]
        + [("hbm", states[0]), ("hbm", states[1]), ("hbm", token)]
        + ([] if first else [("vmem", acc)]),
        [("hbm", states[0].shape, low), ("hbm", states[1].shape, low)]
        + [("hbm", token.shape, token.dtype), ("vmem", (rows2, depth), jnp.float32)]
        + [("hbm", (size, depth), low) for size in sizes],
        {4 + m: 0, 5 + m: 1, 6 + m: 2} | ({} if first else {7 + m: 3}),
        [
            pltpu.VMEM((max(sizes), rows2), jnp.float32),
            pltpu.VMEM((total, rows2), low),
            pltpu.VMEM((total, rows2), low),
            pltpu.VMEM((total, depth), low),
            pltpu.VMEM((total, rows2), low),
            pltpu.VMEM((total, depth), low),
            pltpu.SemaphoreType.DMA((m,)),
            pltpu.SemaphoreType.DMA((2 * m,)),
            pltpu.SemaphoreType.DMA((3 * m,)),
        ],
        limit=26,
    )
    return results[:2], results[2], results[3], results[4:]


def tie(token, *done):
    return call(
        lambda *refs: None,
        [("hbm", value) for value in done] + [("hbm", token)],
        [("hbm", token.shape, token.dtype)],
        {len(done): 0},
        limit=4,
    )[0]


def repeat_body(value, token, token_out, out, sem):
    move = pltpu.make_async_copy(value, out, sem.at[0])
    move.start()
    move.wait()


def repeat(value, token):
    results = call(
        repeat_body,
        [("hbm", value), ("hbm", token)],
        [("hbm", token.shape, token.dtype), ("hbm", value.shape, value.dtype)],
        {1: 0},
        [pltpu.SemaphoreType.DMA((1,))],
        limit=4,
    )
    return results[1], results[0]


def total_body(count, halves, extra, *refs):
    place, terms = refs[0], refs[1 : 1 + count]
    values, result, sem = refs[-3:]
    outs = refs[-5:-3] if halves else refs[-4:-3]
    size, depth = terms[0].shape
    moves = [pltpu.make_async_copy(terms[i], values.at[i], sem.at[i]) for i in range(count)]
    for one in moves:
        one.start()
    for one in moves:
        one.wait()

    @pl.loop(0, size // 16)
    def _(strip):
        here = pl.ds(pl.multiple_of(strip * 16, 16), 16)
        total = values[0, here, :].astype(jnp.float32)
        for i in range(1, count):
            total = total + values[i, here, :].astype(jnp.float32)
        result[here, :] = total.astype(result.dtype)
        if extra:
            tail = pl.ds(depth - LANES, LANES)
            result[here, tail] = (total[:, depth - LANES :] + refs[1 + count][here, :]).astype(result.dtype)

    if halves:
        half = size // 2
        back = [
            pltpu.make_async_copy(
                result.at[pl.ds(pl.multiple_of((place[2] ^ i) * half, 16), half)], outs[i], sem.at[i]
            )
            for i in range(2)
        ]
    else:
        back = [pltpu.make_async_copy(result, outs[0], sem.at[0])]
    for one in back:
        one.start()
    for one in back:
        one.wait()


def total_of(operands, place, token, halves=False, extra=None):
    rows, depth = operands[0].shape
    given = [("smem", place)] + [("hbm", value) for value in operands]
    if extra is not None:
        given.append(("vmem", extra))
    outs = [("hbm", (rows // 2, depth), jnp.bfloat16)] * 2 if halves else [("hbm", (rows, depth), jnp.bfloat16)]
    results = call(
        functools.partial(total_body, len(operands), halves, extra is not None),
        given + [("hbm", token)],
        [("hbm", token.shape, token.dtype)] + outs,
        {len(given): 0},
        [
            pltpu.VMEM((len(operands), rows, depth), jnp.bfloat16),
            pltpu.VMEM((rows, depth), jnp.bfloat16),
            pltpu.SemaphoreType.DMA((len(operands),)),
        ],
        limit=8,
    )
    return (results[1:] if halves else results[1]), results[0]


def finish_body(start, scale, place, mine, other, *refs):
    outs = refs[-6:-4]
    ending, values, result, sem = refs[-4:]
    half, depth = mine.shape
    wide = result.shape[1]
    moves = [
        pltpu.make_async_copy(
            one, values.at[pl.ds(pl.multiple_of((place[2] ^ i) * half, 16), half)], sem.at[i]
        )
        for i, one in enumerate((mine, other))
    ]
    for one in moves:
        one.start()
    for one in moves:
        one.wait()

    @pl.loop(0, 2 * half // 16)
    def _(strip):
        here = pl.ds(pl.multiple_of(strip * 16, 16), 16)
        total = values[here, :].astype(jnp.float32) * scale
        ending[here, :] = total[:, depth - LANES :]
        result[here, :] = total[:, :wide]

    here = pl.ds(start, 2 * half)
    back = [
        pltpu.make_async_copy(result, outs[0].at[here], sem.at[0]),
        pltpu.make_async_copy(ending, outs[1].at[here], sem.at[1]),
    ]
    for one in back:
        one.start()
    for one in back:
        one.wait()


def finish_of(mine, other, results, shapes, start, scale, place, token):
    half, depth = mine.shape
    given = [("smem", place), ("hbm", mine), ("hbm", other)]
    aliases = {len(given): 0}
    given.append(("hbm", token))
    for i, value in enumerate(results):
        aliases[len(given)] = 1 + i
        given.append(("hbm", value))
    outs = call(
        functools.partial(finish_body, start, scale),
        given,
        [("hbm", token.shape, token.dtype)] + [("hbm", one, jnp.float32) for one in shapes],
        aliases,
        [
            pltpu.VMEM((2 * half, LANES), jnp.float32),
            pltpu.VMEM((2 * half, depth), jnp.bfloat16),
            pltpu.VMEM((2 * half, shapes[0][1]), jnp.float32),
            pltpu.SemaphoreType.DMA((2,)),
        ],
        limit=8,
    )
    return outs[1:], outs[0]


def gains_body(acc, plain, token, token_out, gain):
    rows2, depth = plain.shape
    gain[...] = jnp.zeros_like(gain)

    @pl.loop(0, rows2 // 16)
    def _(strip):
        here = pl.ds(pl.multiple_of(strip * 16, 16), 16)
        values = plain[here, :].astype(jnp.float32)
        x_hat = values * lax.rsqrt(jnp.mean(values * values, axis=1, keepdims=True) + 1e-06)
        product = acc[here, :depth] * x_hat
        gain[...] += product[:8] + product[8:]


def gains(acc, plain, token):
    results = call(
        gains_body,
        [("vmem", acc), ("vmem", plain), ("hbm", token)],
        [("hbm", token.shape, token.dtype), ("vmem", (8, plain.shape[1]), jnp.float32)],
        {2: 0},
    )
    return results[1], results[0]


def close_body(acc, state, token, token_out, state_out, own, peer, sem):
    rows = own.shape[0]
    out = [
        pltpu.make_async_copy(acc.at[pl.ds(0, rows)], own, sem.at[0]),
        pltpu.make_async_copy(acc.at[pl.ds(rows, rows)], peer, sem.at[1]),
    ]
    for one in out:
        one.start()
    for one in out:
        one.wait()


def close(acc, state, token):
    rows2, full = acc.shape
    half = ("hbm", (rows2 // 2, full), jnp.float32)
    results = call(
        close_body,
        [("vmem", acc), ("hbm", state), ("hbm", token)],
        [("hbm", token.shape, token.dtype), ("hbm", state.shape, state.dtype), half, half],
        {1: 1, 2: 0},
        [pltpu.SemaphoreType.DMA((2,))],
    )
    return results[1:], results[0]


def pack_body(sizes, weight, bias, token, token_out, *outs):
    depth = weight.shape[1]
    full = outs[0].shape[1]
    lane = lax.broadcasted_iota(jnp.int32, (16, LANES), 1) + (full - LANES)
    start = 0
    for size, out in zip(sizes, outs):
        out[:, :depth] = weight[pl.ds(start, size), :]
        for row in range(0, size, 16):
            column = jnp.broadcast_to(bias[:, start + row : start + row + 16], (LANES, 16)).T
            last = out[row : row + 16, full - LANES :].astype(jnp.float32)
            last = jnp.where(lane < depth, last, jnp.where(lane == depth, column, 0.0))
            out[row : row + 16, full - LANES :] = last.astype(jnp.bfloat16)
        start += size


def pack(weight, bias, token):
    depth = weight.shape[1]
    full = depth + -depth % LANES
    results = call(
        functools.partial(pack_body, CHUNKS),
        [("vmem", weight), ("vmem", bias.astype(jnp.float32)[None, :]), ("hbm", token)],
        [("hbm", token.shape, token.dtype)]
        + [("vmem", (size, full), jnp.bfloat16) for size in CHUNKS],
        {2: 0},
    )
    return results[1:], results[0]


def ranges(units, width):
    for first in range(0, units, LANES):
        at, cuts = first, []
        while at < min(first + LANES, units):
            stop = min(first + LANES, units, (at // width + 1) * width)
            cuts.append((at // width, at % width, at - first, stop - at))
            at = stop
        yield first, cuts


def turn_body(width, place, cot, cot_peer, token, token_out, own, peer):
    core = place[1]
    for source, out in ((cot, own), (cot_peer, peer)):
        for parity in range(2):

            @pl.when(core == parity)
            def _():
                for first, cuts in ranges(source.shape[1], width):
                    cuts = [cut for cut in cuts if cut[0] % 2 == parity]
                    if cuts:
                        block = source[:, first : first + LANES].T
                    for shard, offset, at, size in cuts:
                        to = pl.ds((shard // 2) * width + offset, size)
                        out[to, :] = block[at : at + size]


def turn(cotangent, cot_peer, width, place, token):
    rows, units = cotangent.shape
    half = ("vmem", (units // 2, rows), jnp.bfloat16)
    results = call(
        functools.partial(turn_body, width),
        [("smem", place), ("vmem", cotangent), ("vmem", cot_peer), ("hbm", token)],
        [("hbm", token.shape, token.dtype), half, half],
        {3: 0},
        limit=20,
    )
    return results[1:], results[0]


def back_body(width, place, own, peer, token, token_out, out):
    core = place[1]
    for first, cuts in ranges(out.shape[1], width):
        blocks = []
        for shard, offset, at, size in cuts:
            to = pl.ds((shard // 2) * width + offset, size)
            blocks.append(jnp.where(core == shard % 2, own[to, :], peer[to, :]))
        block = blocks[0] if len(blocks) == 1 else jnp.concatenate(blocks, axis=0)
        out[:, first : first + LANES] = block.T


def back(own, peer, width, place, token):
    units, rows = 2 * own.shape[0], own.shape[1]
    results = call(
        functools.partial(back_body, width),
        [("smem", place), ("vmem", own), ("vmem", peer), ("hbm", token)],
        [("hbm", token.shape, token.dtype), ("vmem", (rows, units), jnp.bfloat16)],
        {3: 0},
    )
    return results[1], results[0]


def norm_body(own, peer, gain, token, token_out, normed, flipped, plain):
    depth, rows = own.shape
    full = normed.shape[1]
    lane = lax.broadcasted_iota(jnp.int32, (LANES, LANES), 1) + (full - LANES)
    for index, source in enumerate((own, peer)):
        for strip in range(0, rows, LANES):
            to = pl.ds(index * rows + strip, LANES)
            for col in range(0, depth, LANES):
                wide = min(LANES, depth - col)
                plain[to, col : col + wide] = source[col : col + wide, strip : strip + LANES].T
            values = plain[to, :].astype(jnp.float32)
            mean_sq = jnp.mean(values * values, axis=1, keepdims=True)
            value = values * lax.rsqrt(mean_sq + 1e-06) * gain[...]
            normed[to, :depth] = value.astype(jnp.bfloat16)
            last = normed[to, full - LANES :]
            last = jnp.where(lane < depth, last, jnp.where(lane == depth, 1.0, 0.0).astype(jnp.bfloat16))
            normed[to, full - LANES :] = last
            for col in range(0, full, LANES):
                flipped[col : col + LANES, to] = normed[to, col : col + LANES].T


def norm(tokens, peer, norm_gain, token):
    depth, rows = tokens.shape
    full = depth + -depth % LANES
    results = call(
        norm_body,
        [("vmem", tokens), ("vmem", peer), ("vmem", norm_gain[None, :]), ("hbm", token)],
        [
            ("hbm", token.shape, token.dtype),
            ("vmem", (2 * rows, full), jnp.bfloat16),
            ("vmem", (full, 2 * rows), jnp.bfloat16),
            ("vmem", (2 * rows, depth), jnp.bfloat16),
        ],
        {3: 0},
        limit=16,
    )
    return results[1:], results[0]


def swap_plane(value, bit=1):
    return lax.ppermute(value, "rep", [(i, i ^ bit) for i in range(4)])


def paired(tokens, norm_gain, up_weight, up_bias, keep_mask, cotangent):
    rows, depth = tokens.shape
    width = up_weight.shape[0]
    index = lax.axis_index("fsdp")
    plane = lax.axis_index("rep")
    place = jnp.stack([index >> 1, index & 1, plane & 1]).astype(jnp.int32)
    inv_root = 1.0 / math.sqrt(rows * 32)
    count = len(CHUNKS)
    starts = [sum(CHUNKS[:c]) for c in range(count)]
    spare = -depth % LANES

    token = jnp.zeros((8, LANES), jnp.float32)
    own, token = pack(up_weight, up_bias, token)
    from_x = [swap_x(piece) for piece in own]
    from_y = [swap_y(piece) for piece in own]
    from_d = [None] * 2 + [swap_x(from_y[c]) if c % 2 == 0 else swap_y(from_x[c]) for c in range(2, count)]

    flat = tokens.T
    (normed, flipped, plain), token = norm(flat, swap_core(flat), norm_gain, token)
    scale_own = row_scales(keep_mask, rows)
    scale = jnp.concatenate([scale_own, swap_core(scale_own)])[None, :]
    states, token = turn(cotangent, swap_core(cotangent), width, place, token)

    pieces = {}
    for c in range(count):
        pieces["O", c], pieces["X", c], pieces["Y", c] = own[c], from_x[c], from_y[c]
        pieces["D", c] = from_d[c]
    side = {"O": 0, "X": 1, "Y": 2, "D": 3}
    grads, sent_x, sent_y, relayed = {}, {}, {}, {}
    kept, across, results, acc = {}, {}, (), None
    hidden = grad_in = None

    def run(keys):
        nonlocal states, token, acc
        spots = [(starts[c], side[kind]) for kind, c in keys]
        states, token, acc, grad = work(
            [pieces[key] for key in keys], spots, width, place, normed, flipped, scale, states, token, acc
        )
        grads.update(zip(keys, grad))

    for task in "".join(ORDER).split():
        kind, c = task[0], int(task[1:]) if task[1:].isdigit() else 0
        even = c % 2 == 0
        if kind == "W":
            run([("X", c), ("Y", c)])
            if even:
                sent_y[c] = swap_y(grads["Y", c])
            else:
                sent_x[c] = swap_x(grads["X", c])
        elif kind == "B":
            run([("D", c)])
            relayed[c] = swap_y(grads["D", c]) if even else swap_x(grads["D", c])
        elif kind == "O":
            run([("O", k) for k in (range(2) if task == "Oa" else range(2, count))])
        elif kind == "r":
            value, token = repeat(from_y[c] if even else from_x[c], token)
            pieces["D", c] = swap_x(value) if even else swap_y(value)
        elif kind == "R":
            value, token = total_of([grads["X" if even else "Y", c], relayed[c]], place, token)
            if even:
                sent_x[c] = swap_x(value)
            else:
                sent_y[c] = swap_y(value)
        elif kind == "S":
            extra = None
            if c == count - 1:
                lanes = gain.reshape(depth // 32, 32)
                extra = jnp.pad(lanes, ((0, CHUNKS[c] - depth // 32), (LANES - 32, 0)))
            terms = [grads["O", c], sent_x[c], sent_y[c]]
            (kept[c], other), token = total_of(terms, place, token, True, extra)
            across[c] = swap_plane(other, 1)
        elif kind == "T":
            kept[c], token = total_of([kept[c], across[c]], place, token)
            across[c] = swap_plane(kept[c], 2)
        elif kind == "V":
            kept[c], token = total_of([kept[c], across[c]], place, token)
            across[c] = swap_plane(kept[c], 1)
        elif kind == "U":
            shapes = [(width, depth), (width, LANES)]
            results, token = finish_of(
                kept[c], across[c], results, shapes, starts[c], inv_root, place, token
            )
        elif kind == "G":
            gain, token = gains(acc, plain, token)
            gain = jnp.sum(gain, axis=0)
            gain = gain + swap_core(gain)
        elif kind == "g":
            token = tie(token, gain)
            if task == "ga":
                gain = gain + swap_x(gain)
            elif task == "gb":
                gain = gain + swap_y(gain)
        elif kind == "K":
            (state, whole, peer), token = close(acc, states[1], token)
            state, peer = swap_core(state), swap_core(peer)
        elif kind == "H":
            hidden, token = back(states[0], state, width, place, token)
        elif kind == "J":
            x_hat, inv_rms, _ = normalize(plain[:rows], norm_gain)
            scaled = (whole + peer)[:, :depth] * norm_gain[None, :]
            grad_in = (
                inv_rms * (scaled - x_hat * jnp.mean(scaled * x_hat, axis=1, keepdims=True))
            ).astype(jnp.bfloat16)
            token = tie(token, grad_in)

    grad_weight, tail = results
    grad_bias = tail[:, LANES - spare]
    grad_gain = tail[starts[-1] : starts[-1] + depth // 32, LANES - 32 :].reshape(depth)
    return (hidden, grad_in, grad_weight, grad_bias, grad_gain)


def local(tokens, norm_gain, up_weight, up_bias, keep_mask, cotangent):
    x_hat, inv_rms, normed = normalize(tokens, norm_gain)
    rows = tokens.shape[0]
    width = up_weight.shape[0]
    tok_total = rows * lax.axis_size("fsdp") * lax.axis_size("rep")
    inv_root = 1.0 / math.sqrt(tok_total)
    weight_all, bias_all = (
        lax.all_gather(up_weight, "fsdp", axis=0, tiled=True),
        lax.all_gather(up_bias, "fsdp", axis=0, tiled=True),
    )
    scales = row_scales(keep_mask, rows)[:, None]
    preact = contract_last(normed, weight_all) + bias_all.astype(jnp.float32)[None, :]
    gelu_out, slopes = activate(preact)
    hidden = (gelu_out * scales).astype(jnp.bfloat16)
    grad_pre = cotangent.astype(jnp.float32) * scales * slopes
    grad_low = grad_pre.astype(jnp.bfloat16)
    weight_part = lax.psum_scatter(
        lax.dot_general(
            grad_low, normed, (((0,), (0,)), ((), ())), preferred_element_type=jnp.float32
        ).astype(jnp.bfloat16),
        "fsdp",
        scatter_dimension=0,
        tiled=True,
    )
    weight_sum = lax.psum(weight_part, "rep").astype(jnp.float32)
    grad_norm = jnp.dot(grad_low, weight_all, preferred_element_type=jnp.float32)
    bias_total, gain_total = lax.psum(
        (jnp.sum(grad_pre, axis=0), jnp.sum(grad_norm * x_hat, axis=0)), ("fsdp", "rep")
    )
    bias_sum = lax.dynamic_slice_in_dim(bias_total, lax.axis_index("fsdp") * width, width, 0)
    scaled = grad_norm * norm_gain[None, :]
    grad_in = (inv_rms * (scaled - x_hat * jnp.mean(scaled * x_hat, axis=1, keepdims=True))).astype(
        jnp.bfloat16
    )
    return (hidden, grad_in, weight_sum * inv_root, bias_sum * inv_root, gain_total * inv_root)


def solution(mesh):
    body = paired if (mesh.shape["fsdp"], mesh.shape["rep"]) == (8, 4) else local
    return jax.shard_map(
        body,
        mesh=mesh,
        in_specs=(
            P(("fsdp", "rep"), None),
            P(),
            P("fsdp", None),
            P("fsdp"),
            P(("fsdp", "rep")),
            P(("fsdp", "rep"), None),
        ),
        out_specs=(
            P(("fsdp", "rep"), None),
            P(("fsdp", "rep"), None),
            P("fsdp", None),
            P("fsdp"),
            P(),
        ),
        check_vma=False,
    )
```

```python
import functools
import math

import jax
import jax.numpy as jnp
from jax import lax
from jax.experimental import pallas as pl
from jax.experimental.pallas import tpu as pltpu
from jax.sharding import PartitionSpec as P

CHUNKS = (192, 192, 160, 160, 96)
ORDER = (
    "Oa r0 W0 r1 ",
    "W1 B0 B1 W2 ",
    "B2 R0 R1 Ob ",
    "S0 S1 T0 W3 ",
    "B3 W4 V0 T1 ",
    "R2 B4 R3 U0 ",
    "G S2 V1 R4 ",
    "T2 ga S3 U1 ",
    "gb V2 gd T3 ",
    "S4 V3 T4 U2 ",
    "K V4 H J ",
    "U3 U4 ",
)


def normalize(tokens, norm_gain):
    values = tokens.astype(jnp.float32)
    mean_sq = jnp.mean(values * values, axis=1, keepdims=True)
    inv_rms = lax.rsqrt(mean_sq + 1e-06)
    x_hat = values * inv_rms
    return (x_hat, inv_rms, (x_hat * norm_gain[None, :]).astype(jnp.bfloat16))


def activate(preact):
    cdf = 0.5 * (1.0 + jax.scipy.special.erf(preact * 0.7071067811865476))
    density = jnp.exp(-0.5 * preact * preact) * 0.3989422804014327
    return (preact * cdf, cdf + preact * density)


def row_scales(keep_mask, total_rows):
    per_sample = keep_mask.astype(jnp.float32) * (4.0 / 3.0)
    return jnp.repeat(per_sample, total_rows // keep_mask.shape[0])


def contract_last(left, right):
    return lax.dot_general(
        left, right, (((1,), (1,)), ((), ())), preferred_element_type=jnp.float32
    )


def swap(value, bit):
    return lax.ppermute(value, "fsdp", [(i, i ^ bit) for i in range(8)])


def swap_core(value):
    return swap(value, 1)


def swap_x(value):
    return swap(value, 2)


def swap_y(value):
    return swap(value, 4)


LANES = 128


def work_body(sizes, spots, width, first, *refs):
    m = len(sizes)
    place, normed, flipped, scale = refs[:4]
    piece_hbm = refs[4 : 4 + m]
    outs = refs[4 + m + 3 + (not first) :]
    former = None if first else refs[4 + m + 3]
    states, acc, grad_hbm = outs[:2], outs[3], outs[4 : 4 + m]
    pre, cot, hid, piece_v, low_v, grad_v, in_sem, cot_sem, out_sem = outs[4 + m :]
    rows2 = normed.shape[0]
    rows = rows2 // 2
    depth = normed.shape[1]
    begin = [sum(sizes[:j]) for j in range(m)]

    def near(j):
        return pl.ds(begin[j], sizes[j])

    def spot(j):
        start, side = spots[j]
        return pl.ds(pl.multiple_of(start + width * (place[0] ^ side), 16), sizes[j])

    copy = pltpu.make_async_copy
    piece_in = [copy(piece_hbm[j], piece_v.at[near(j)], in_sem.at[j]) for j in range(m)]
    cot_in = [
        copy(states[i].at[spot(j)], cot.at[near(j), pl.ds(i * rows, rows)], cot_sem.at[2 * j + i])
        for j in range(m)
        for i in range(2)
    ]
    hid_out = [
        copy(hid.at[near(j), pl.ds(i * rows, rows)], states[i].at[spot(j)], out_sem.at[3 * j + i])
        for j in range(m)
        for i in range(2)
    ]
    grad_out = [copy(grad_v.at[near(j)], grad_hbm[j], out_sem.at[3 * j + 2]) for j in range(m)]

    for j in range(m):
        piece_in[j].start()
        for one in cot_in[2 * j : 2 * j + 2]:
            one.start()
    for j in range(m):
        size = sizes[j]
        piece_in[j].wait()
        pre[:size, :] = jnp.dot(piece_v[near(j), :], flipped[...], preferred_element_type=jnp.float32)
        for one in cot_in[2 * j : 2 * j + 2]:
            one.wait()

        @pl.loop(0, size // 16)
        def _(strip):
            here = pl.ds(pl.multiple_of(strip * 16, 16), 16)
            there = pl.ds(pl.multiple_of(begin[j] + strip * 16, 16), 16)
            for col in range(0, rows2, 2 * LANES):
                cols = pl.ds(col, 2 * LANES)
                gelu_out, slopes = activate(pre[here, cols])
                factor = scale[:, cols]
                hid[there, cols] = (gelu_out * factor).astype(jnp.bfloat16)
                grad = cot[there, cols].astype(jnp.float32) * factor * slopes
                low_v[there, cols] = grad.astype(jnp.bfloat16)

        for one in hid_out[2 * j : 2 * j + 2]:
            one.start()
        for col in range(0, depth, 4 * LANES):
            cols = pl.ds(col, min(4 * LANES, depth - col))
            grad_v[near(j), cols] = jnp.dot(
                low_v[near(j), :], normed[:, cols], preferred_element_type=jnp.float32
            ).astype(jnp.bfloat16)
        grad_out[j].start()
    turned = low_v[...].T
    for col in range(0, depth, 4 * LANES):
        cols = pl.ds(col, min(4 * LANES, depth - col))
        part = jnp.dot(turned, piece_v[:, cols], preferred_element_type=jnp.float32)
        acc[:, cols] = part if first else former[:, cols] + part
    for one in hid_out + grad_out:
        one.wait()


def call(body, operands, outs, aliases, scratch=(), limit=16):
    spec = {
        "hbm": pl.BlockSpec(memory_space=pltpu.HBM),
        "vmem": pl.BlockSpec(memory_space=pltpu.VMEM),
        "smem": pl.BlockSpec(memory_space=pltpu.SMEM),
    }
    return pl.pallas_call(
        body,
        out_shape=[jax.ShapeDtypeStruct(shape, dtype) for _, shape, dtype in outs],
        in_specs=[spec[space] for space, _ in operands],
        out_specs=[spec[space] for space, _, _ in outs],
        scratch_shapes=list(scratch),
        input_output_aliases=aliases,
        compiler_params=pltpu.CompilerParams(vmem_limit_bytes=limit * 1024 * 1024),
        cost_estimate=pl.CostEstimate(flops=0, bytes_accessed=0, transcendentals=0),
    )(*[value for _, value in operands])


def work(pieces, spots, width, place, normed, flipped, scale, states, token, acc):
    sizes = [piece.shape[0] for piece in pieces]
    m, total = len(sizes), sum(sizes)
    rows2, depth = normed.shape
    low = jnp.bfloat16
    first = acc is None
    results = call(
        functools.partial(work_body, sizes, spots, width, first),
        [("smem", place), ("vmem", normed), ("vmem", flipped), ("vmem", scale)]
        + [("hbm", piece) for piece in pieces]
        + [("hbm", states[0]), ("hbm", states[1]), ("hbm", token)]
        + ([] if first else [("vmem", acc)]),
        [("hbm", states[0].shape, low), ("hbm", states[1].shape, low)]
        + [("hbm", token.shape, token.dtype), ("vmem", (rows2, depth), jnp.float32)]
        + [("hbm", (size, depth), low) for size in sizes],
        {4 + m: 0, 5 + m: 1, 6 + m: 2} | ({} if first else {7 + m: 3}),
        [
            pltpu.VMEM((max(sizes), rows2), jnp.float32),
            pltpu.VMEM((total, rows2), low),
            pltpu.VMEM((total, rows2), low),
            pltpu.VMEM((total, depth), low),
            pltpu.VMEM((total, rows2), low),
            pltpu.VMEM((total, depth), low),
            pltpu.SemaphoreType.DMA((m,)),
            pltpu.SemaphoreType.DMA((2 * m,)),
            pltpu.SemaphoreType.DMA((3 * m,)),
        ],
        limit=26,
    )
    return results[:2], results[2], results[3], results[4:]


def tie(token, *done):
    return call(
        lambda *refs: None,
        [("hbm", value) for value in done] + [("hbm", token)],
        [("hbm", token.shape, token.dtype)],
        {len(done): 0},
        limit=4,
    )[0]


def repeat_body(value, token, token_out, out, sem):
    move = pltpu.make_async_copy(value, out, sem.at[0])
    move.start()
    move.wait()


def repeat(value, token):
    results = call(
        repeat_body,
        [("hbm", value), ("hbm", token)],
        [("hbm", token.shape, token.dtype), ("hbm", value.shape, value.dtype)],
        {1: 0},
        [pltpu.SemaphoreType.DMA((1,))],
        limit=4,
    )
    return results[1], results[0]


def total_body(count, halves, extra, *refs):
    place, terms = refs[0], refs[1 : 1 + count]
    values, result, sem = refs[-3:]
    outs = refs[-5:-3] if halves else refs[-4:-3]
    size, depth = terms[0].shape
    moves = [pltpu.make_async_copy(terms[i], values.at[i], sem.at[i]) for i in range(count)]
    for one in moves:
        one.start()
    for one in moves:
        one.wait()

    @pl.loop(0, size // 16)
    def _(strip):
        here = pl.ds(pl.multiple_of(strip * 16, 16), 16)
        total = values[0, here, :].astype(jnp.float32)
        for i in range(1, count):
            total = total + values[i, here, :].astype(jnp.float32)
        result[here, :] = total.astype(result.dtype)
        if extra:
            tail = pl.ds(depth - LANES, LANES)
            result[here, tail] = (total[:, depth - LANES :] + refs[1 + count][here, :]).astype(result.dtype)

    if halves:
        half = size // 2
        back = [
            pltpu.make_async_copy(
                result.at[pl.ds(pl.multiple_of((place[2] ^ i) * half, 16), half)], outs[i], sem.at[i]
            )
            for i in range(2)
        ]
    else:
        back = [pltpu.make_async_copy(result, outs[0], sem.at[0])]
    for one in back:
        one.start()
    for one in back:
        one.wait()


def total_of(operands, place, token, halves=False, extra=None):
    rows, depth = operands[0].shape
    given = [("smem", place)] + [("hbm", value) for value in operands]
    if extra is not None:
        given.append(("vmem", extra))
    outs = [("hbm", (rows // 2, depth), jnp.bfloat16)] * 2 if halves else [("hbm", (rows, depth), jnp.bfloat16)]
    results = call(
        functools.partial(total_body, len(operands), halves, extra is not None),
        given + [("hbm", token)],
        [("hbm", token.shape, token.dtype)] + outs,
        {len(given): 0},
        [
            pltpu.VMEM((len(operands), rows, depth), jnp.bfloat16),
            pltpu.VMEM((rows, depth), jnp.bfloat16),
            pltpu.SemaphoreType.DMA((len(operands),)),
        ],
        limit=8,
    )
    return (results[1:] if halves else results[1]), results[0]


def finish_body(start, scale, place, mine, other, *refs):
    outs = refs[-6:-4]
    ending, values, result, sem = refs[-4:]
    half, depth = mine.shape
    wide = result.shape[1]
    moves = [
        pltpu.make_async_copy(
            one, values.at[pl.ds(pl.multiple_of((place[2] ^ i) * half, 16), half)], sem.at[i]
        )
        for i, one in enumerate((mine, other))
    ]
    for one in moves:
        one.start()
    for one in moves:
        one.wait()

    @pl.loop(0, 2 * half // 16)
    def _(strip):
        here = pl.ds(pl.multiple_of(strip * 16, 16), 16)
        total = values[here, :].astype(jnp.float32) * scale
        ending[here, :] = total[:, depth - LANES :]
        result[here, :] = total[:, :wide]

    here = pl.ds(start, 2 * half)
    back = [
        pltpu.make_async_copy(result, outs[0].at[here], sem.at[0]),
        pltpu.make_async_copy(ending, outs[1].at[here], sem.at[1]),
    ]
    for one in back:
        one.start()
    for one in back:
        one.wait()


def finish_of(mine, other, results, shapes, start, scale, place, token):
    half, depth = mine.shape
    given = [("smem", place), ("hbm", mine), ("hbm", other)]
    aliases = {len(given): 0}
    given.append(("hbm", token))
    for i, value in enumerate(results):
        aliases[len(given)] = 1 + i
        given.append(("hbm", value))
    outs = call(
        functools.partial(finish_body, start, scale),
        given,
        [("hbm", token.shape, token.dtype)] + [("hbm", one, jnp.float32) for one in shapes],
        aliases,
        [
            pltpu.VMEM((2 * half, LANES), jnp.float32),
            pltpu.VMEM((2 * half, depth), jnp.bfloat16),
            pltpu.VMEM((2 * half, shapes[0][1]), jnp.float32),
            pltpu.SemaphoreType.DMA((2,)),
        ],
        limit=8,
    )
    return outs[1:], outs[0]


def gains_body(acc, plain, token, token_out, gain):
    rows2, depth = plain.shape
    gain[...] = jnp.zeros_like(gain)

    @pl.loop(0, rows2 // 16)
    def _(strip):
        here = pl.ds(pl.multiple_of(strip * 16, 16), 16)
        values = plain[here, :].astype(jnp.float32)
        x_hat = values * lax.rsqrt(jnp.mean(values * values, axis=1, keepdims=True) + 1e-06)
        product = acc[here, :depth] * x_hat
        gain[...] += product[:8] + product[8:]


def gains(acc, plain, token):
    results = call(
        gains_body,
        [("vmem", acc), ("vmem", plain), ("hbm", token)],
        [("hbm", token.shape, token.dtype), ("vmem", (8, plain.shape[1]), jnp.float32)],
        {2: 0},
    )
    return results[1], results[0]


def close_body(acc, state, token, token_out, state_out, own, peer, sem):
    rows = own.shape[0]
    out = [
        pltpu.make_async_copy(acc.at[pl.ds(0, rows)], own, sem.at[0]),
        pltpu.make_async_copy(acc.at[pl.ds(rows, rows)], peer, sem.at[1]),
    ]
    for one in out:
        one.start()
    for one in out:
        one.wait()


def close(acc, state, token):
    rows2, full = acc.shape
    half = ("hbm", (rows2 // 2, full), jnp.float32)
    results = call(
        close_body,
        [("vmem", acc), ("hbm", state), ("hbm", token)],
        [("hbm", token.shape, token.dtype), ("hbm", state.shape, state.dtype), half, half],
        {1: 1, 2: 0},
        [pltpu.SemaphoreType.DMA((2,))],
    )
    return results[1:], results[0]


def pack_body(sizes, weight, bias, token, token_out, *outs):
    depth = weight.shape[1]
    full = outs[0].shape[1]
    lane = lax.broadcasted_iota(jnp.int32, (16, LANES), 1) + (full - LANES)
    start = 0
    for size, out in zip(sizes, outs):
        out[:, :depth] = weight[pl.ds(start, size), :]
        for row in range(0, size, 16):
            column = jnp.broadcast_to(bias[:, start + row : start + row + 16], (LANES, 16)).T
            last = out[row : row + 16, full - LANES :].astype(jnp.float32)
            last = jnp.where(lane < depth, last, jnp.where(lane == depth, column, 0.0))
            out[row : row + 16, full - LANES :] = last.astype(jnp.bfloat16)
        start += size


def pack(weight, bias, token):
    depth = weight.shape[1]
    full = depth + -depth % LANES
    results = call(
        functools.partial(pack_body, CHUNKS),
        [("vmem", weight), ("vmem", bias.astype(jnp.float32)[None, :]), ("hbm", token)],
        [("hbm", token.shape, token.dtype)]
        + [("vmem", (size, full), jnp.bfloat16) for size in CHUNKS],
        {2: 0},
    )
    return results[1:], results[0]


def ranges(units, width):
    for first in range(0, units, LANES):
        at, cuts = first, []
        while at < min(first + LANES, units):
            stop = min(first + LANES, units, (at // width + 1) * width)
            cuts.append((at // width, at % width, at - first, stop - at))
            at = stop
        yield first, cuts


def turn_body(width, place, cot, cot_peer, token, token_out, own, peer):
    core = place[1]
    for source, out in ((cot, own), (cot_peer, peer)):
        for parity in range(2):

            @pl.when(core == parity)
            def _():
                for first, cuts in ranges(source.shape[1], width):
                    cuts = [cut for cut in cuts if cut[0] % 2 == parity]
                    if cuts:
                        block = source[:, first : first + LANES].T
                    for shard, offset, at, size in cuts:
                        to = pl.ds((shard // 2) * width + offset, size)
                        out[to, :] = block[at : at + size]


def turn(cotangent, cot_peer, width, place, token):
    rows, units = cotangent.shape
    half = ("vmem", (units // 2, rows), jnp.bfloat16)
    results = call(
        functools.partial(turn_body, width),
        [("smem", place), ("vmem", cotangent), ("vmem", cot_peer), ("hbm", token)],
        [("hbm", token.shape, token.dtype), half, half],
        {3: 0},
        limit=20,
    )
    return results[1:], results[0]


def back_body(width, place, own, peer, token, token_out, out):
    core = place[1]
    for first, cuts in ranges(out.shape[1], width):
        blocks = []
        for shard, offset, at, size in cuts:
            to = pl.ds((shard // 2) * width + offset, size)
            blocks.append(jnp.where(core == shard % 2, own[to, :], peer[to, :]))
        block = blocks[0] if len(blocks) == 1 else jnp.concatenate(blocks, axis=0)
        out[:, first : first + LANES] = block.T


def back(own, peer, width, place, token):
    units, rows = 2 * own.shape[0], own.shape[1]
    results = call(
        functools.partial(back_body, width),
        [("smem", place), ("vmem", own), ("vmem", peer), ("hbm", token)],
        [("hbm", token.shape, token.dtype), ("vmem", (rows, units), jnp.bfloat16)],
        {3: 0},
    )
    return results[1], results[0]


def norm_body(own, peer, gain, token, token_out, normed, flipped, plain):
    depth, rows = own.shape
    full = normed.shape[1]
    lane = lax.broadcasted_iota(jnp.int32, (LANES, LANES), 1) + (full - LANES)
    for index, source in enumerate((own, peer)):
        for strip in range(0, rows, LANES):
            to = pl.ds(index * rows + strip, LANES)
            for col in range(0, depth, LANES):
                wide = min(LANES, depth - col)
                plain[to, col : col + wide] = source[col : col + wide, strip : strip + LANES].T
            values = plain[to, :].astype(jnp.float32)
            mean_sq = jnp.mean(values * values, axis=1, keepdims=True)
            value = values * lax.rsqrt(mean_sq + 1e-06) * gain[...]
            normed[to, :depth] = value.astype(jnp.bfloat16)
            last = normed[to, full - LANES :]
            last = jnp.where(lane < depth, last, jnp.where(lane == depth, 1.0, 0.0).astype(jnp.bfloat16))
            normed[to, full - LANES :] = last
            for col in range(0, full, LANES):
                flipped[col : col + LANES, to] = normed[to, col : col + LANES].T


def norm(tokens, peer, norm_gain, token):
    depth, rows = tokens.shape
    full = depth + -depth % LANES
    results = call(
        norm_body,
        [("vmem", tokens), ("vmem", peer), ("vmem", norm_gain[None, :]), ("hbm", token)],
        [
            ("hbm", token.shape, token.dtype),
            ("vmem", (2 * rows, full), jnp.bfloat16),
            ("vmem", (full, 2 * rows), jnp.bfloat16),
            ("vmem", (2 * rows, depth), jnp.bfloat16),
        ],
        {3: 0},
        limit=16,
    )
    return results[1:], results[0]


def swap_plane(value, bit=1):
    return lax.ppermute(value, "rep", [(i, i ^ bit) for i in range(4)])


def paired(tokens, norm_gain, up_weight, up_bias, keep_mask, cotangent):
    rows, depth = tokens.shape
    width = up_weight.shape[0]
    index = lax.axis_index("fsdp")
    plane = lax.axis_index("rep")
    place = jnp.stack([index >> 1, index & 1, plane & 1]).astype(jnp.int32)
    inv_root = 1.0 / math.sqrt(rows * 32)
    count = len(CHUNKS)
    starts = [sum(CHUNKS[:c]) for c in range(count)]
    spare = -depth % LANES

    token = jnp.zeros((8, LANES), jnp.float32)
    own, token = pack(up_weight, up_bias, token)
    from_x = [swap_x(piece) for piece in own]
    from_y = [swap_y(piece) for piece in own]
    from_d = [None] * 2 + [swap_x(from_y[c]) if c % 2 == 0 else swap_y(from_x[c]) for c in range(2, count)]

    flat = tokens.T
    (normed, flipped, plain), token = norm(flat, swap_core(flat), norm_gain, token)
    scale_own = row_scales(keep_mask, rows)
    scale = jnp.concatenate([scale_own, swap_core(scale_own)])[None, :]
    states, token = turn(cotangent, swap_core(cotangent), width, place, token)

    pieces = {}
    for c in range(count):
        pieces["O", c], pieces["X", c], pieces["Y", c] = own[c], from_x[c], from_y[c]
        pieces["D", c] = from_d[c]
    side = {"O": 0, "X": 1, "Y": 2, "D": 3}
    grads, sent_x, sent_y, relayed = {}, {}, {}, {}
    kept, across, results, acc = {}, {}, (), None
    hidden = grad_in = None

    def run(keys):
        nonlocal states, token, acc
        spots = [(starts[c], side[kind]) for kind, c in keys]
        states, token, acc, grad = work(
            [pieces[key] for key in keys], spots, width, place, normed, flipped, scale, states, token, acc
        )
        grads.update(zip(keys, grad))

    for task in "".join(ORDER).split():
        kind, c = task[0], int(task[1:]) if task[1:].isdigit() else 0
        even = c % 2 == 0
        if kind == "W":
            run([("X", c), ("Y", c)])
            if even:
                sent_y[c] = swap_y(grads["Y", c])
            else:
                sent_x[c] = swap_x(grads["X", c])
        elif kind == "B":
            run([("D", c)])
            relayed[c] = swap_y(grads["D", c]) if even else swap_x(grads["D", c])
        elif kind == "O":
            run([("O", k) for k in (range(2) if task == "Oa" else range(2, count))])
        elif kind == "r":
            value, token = repeat(from_y[c] if even else from_x[c], token)
            pieces["D", c] = swap_x(value) if even else swap_y(value)
        elif kind == "R":
            value, token = total_of([grads["X" if even else "Y", c], relayed[c]], place, token)
            if even:
                sent_x[c] = swap_x(value)
            else:
                sent_y[c] = swap_y(value)
        elif kind == "S":
            extra = None
            if c == count - 1:
                lanes = gain.reshape(depth // 32, 32)
                extra = jnp.pad(lanes, ((0, CHUNKS[c] - depth // 32), (LANES - 32, 0)))
            terms = [grads["O", c], sent_x[c], sent_y[c]]
            (kept[c], other), token = total_of(terms, place, token, True, extra)
            across[c] = swap_plane(other, 1)
        elif kind == "T":
            kept[c], token = total_of([kept[c], across[c]], place, token)
            across[c] = swap_plane(kept[c], 2)
        elif kind == "V":
            kept[c], token = total_of([kept[c], across[c]], place, token)
            across[c] = swap_plane(kept[c], 1)
        elif kind == "U":
            shapes = [(width, depth), (width, LANES)]
            results, token = finish_of(
                kept[c], across[c], results, shapes, starts[c], inv_root, place, token
            )
        elif kind == "G":
            gain, token = gains(acc, plain, token)
            gain = jnp.sum(gain, axis=0)
            gain = gain + swap_core(gain)
        elif kind == "g":
            token = tie(token, gain)
            if task == "ga":
                gain = gain + swap_x(gain)
            elif task == "gb":
                gain = gain + swap_y(gain)
        elif kind == "K":
            (state, whole, peer), token = close(acc, states[1], token)
            state, peer = swap_core(state), swap_core(peer)
        elif kind == "H":
            hidden, token = back(states[0], state, width, place, token)
        elif kind == "J":
            x_hat, inv_rms, _ = normalize(plain[:rows], norm_gain)
            scaled = (whole + peer)[:, :depth] * norm_gain[None, :]
            grad_in = (
                inv_rms * (scaled - x_hat * jnp.mean(scaled * x_hat, axis=1, keepdims=True))
            ).astype(jnp.bfloat16)
            token = tie(token, grad_in)

    grad_weight, tail = results
    grad_bias = tail[:, LANES - spare]
    grad_gain = tail[starts[-1] : starts[-1] + depth // 32, LANES - 32 :].reshape(depth)
    return (hidden, grad_in, grad_weight, grad_bias, grad_gain)


def local(tokens, norm_gain, up_weight, up_bias, keep_mask, cotangent):
    x_hat, inv_rms, normed = normalize(tokens, norm_gain)
    rows = tokens.shape[0]
    width = up_weight.shape[0]
    tok_total = rows * lax.axis_size("fsdp") * lax.axis_size("rep")
    inv_root = 1.0 / math.sqrt(tok_total)
    weight_all, bias_all = (
        lax.all_gather(up_weight, "fsdp", axis=0, tiled=True),
        lax.all_gather(up_bias, "fsdp", axis=0, tiled=True),
    )
    scales = row_scales(keep_mask, rows)[:, None]
    preact = contract_last(normed, weight_all) + bias_all.astype(jnp.float32)[None, :]
    gelu_out, slopes = activate(preact)
    hidden = (gelu_out * scales).astype(jnp.bfloat16)
    grad_pre = cotangent.astype(jnp.float32) * scales * slopes
    grad_low = grad_pre.astype(jnp.bfloat16)
    weight_part = lax.psum_scatter(
        lax.dot_general(
            grad_low, normed, (((0,), (0,)), ((), ())), preferred_element_type=jnp.float32
        ).astype(jnp.bfloat16),
        "fsdp",
        scatter_dimension=0,
        tiled=True,
    )
    weight_sum = lax.psum(weight_part, "rep").astype(jnp.float32)
    grad_norm = jnp.dot(grad_low, weight_all, preferred_element_type=jnp.float32)
    bias_total, gain_total = lax.psum(
        (jnp.sum(grad_pre, axis=0), jnp.sum(grad_norm * x_hat, axis=0)), ("fsdp", "rep")
    )
    bias_sum = lax.dynamic_slice_in_dim(bias_total, lax.axis_index("fsdp") * width, width, 0)
    scaled = grad_norm * norm_gain[None, :]
    grad_in = (inv_rms * (scaled - x_hat * jnp.mean(scaled * x_hat, axis=1, keepdims=True))).astype(
        jnp.bfloat16
    )
    return (hidden, grad_in, weight_sum * inv_root, bias_sum * inv_root, gain_total * inv_root)


def solution(mesh):
    body = paired if (mesh.shape["fsdp"], mesh.shape["rep"]) == (8, 4) else local
    return jax.shard_map(
        body,
        mesh=mesh,
        in_specs=(
            P(("fsdp", "rep"), None),
            P(),
            P("fsdp", None),
            P("fsdp"),
            P(("fsdp", "rep")),
            P(("fsdp", "rep"), None),
        ),
        out_specs=(
            P(("fsdp", "rep"), None),
            P(("fsdp", "rep"), None),
            P("fsdp", None),
            P("fsdp"),
            P(),
        ),
        check_vma=False,
    )
```
